256 devices in a mesh: rep: 8 (over y, core), shard: 32 (over x, z).
Axes of the slice: x: 4, y: 4, z: 8, core: 2. Of those that a mesh axis runs over, the one named last changes fastest.
Arguments:
- tokens: bfloat16 [114688, 12288], P(('rep', 'shard')), may hold values from -60 to 60
- cotangent: bfloat16 [114688, 256], P(('rep', 'shard')), may hold values from -40 to 40
- master: float32 [12288, 256], P('shard'), may hold values from -4 to 4
- first_moment: float32 [12288, 256], P('shard'), may hold values from -3 to 3
- second_moment: float32 [12288, 256], P('shard'), may hold values from 0.05 to 2
Outputs:
- master_new: float32 [12288, 256], P('shard')
- first_new: float32 [12288, 256], P('shard')
- second_new: float32 [12288, 256], P('shard')
- activations: bfloat16 [114688, 256], P(('rep', 'shard'))
The draws below stay inside these ranges and needn't reach their ends.
All inputs are finite; a program needn't handle non-finite values.
Results may differ from the reference program's by a relative error of at most 0.015.
Values may be sent and summed in bfloat16 or wider, within the bound.
No kernel may reach another device: no remote copies, remote signals or barrier semaphores. Data moves between devices by JAX's collectives and lax.ppermute only.
A program may use at most 64 MiB of HBM per device.

```python
import math
import jax
import jax.numpy as jnp
from jax import lax

D = 12288
COLS = 256
TOK_DEV = 448
STEP = 10
TOKENS = 114688
N_REP = 8
N_SHARD = 32


def draw_tokens(key, part):
    key = jax.random.fold_in(key, 11)
    key_base, key_cols = jax.random.split(key, 2)
    position = jnp.arange(D, dtype=jnp.float32) / D
    column_scale = (1.0 + 2.0 * position) / 3.0 * 10.0 ** jax.random.uniform(key_cols, (D,), jnp.float32)
    base = jax.random.truncated_normal(key_base, -4.0, 4.0, (TOKENS, D), jnp.float32)
    return (base * column_scale).astype(jnp.bfloat16)


def draw_cotangent(key, part):
    key = jax.random.fold_in(key, 23)
    key_base, key_cols = jax.random.split(key, 2)
    column_scale = 10.0 ** jax.random.uniform(key_cols, (COLS,), jnp.float32)
    base = jax.random.truncated_normal(key_base, -4.0, 4.0, (TOKENS, COLS), jnp.float32)
    return (base * column_scale).astype(jnp.bfloat16)


def levels(rng, shape, cuts, smallest, high):
    loudness, own = 1.0, jax.random.fold_in(rng, 6)
    for axis_at, shards_of in cuts:
        heights = jnp.exp(jax.random.uniform(jax.random.fold_in(own, axis_at), (shards_of,), jnp.float32, smallest / len(cuts), high / len(cuts)))
        loudness = loudness * jnp.repeat(heights, shape[axis_at] // shards_of).reshape([-1 if axis == axis_at else 1 for axis in range(len(shape))])
    return loudness


def centred(key, shape, width, limit, cuts=(), kind=jnp.bfloat16):
    loudness = levels(key, shape, cuts, -0.22, 0.18) if cuts else 1.0
    entries = jax.random.normal(key, shape, jnp.float32) * width * loudness
    return jnp.minimum(jnp.maximum(entries, -limit), limit).astype(kind)


def setup_inputs(seed: int = 0) -> dict:
    key_list = jax.random.split(jax.random.key(seed), 6)
    return {
        "tokens": draw_tokens(jax.random.fold_in(key_list[5], 71), 0),
        "cotangent": draw_cotangent(jax.random.fold_in(key_list[5], 71), 0),
        "master": centred(key_list[2], (D, COLS), 1.0, 4.0, ((0, 32),), jnp.float32),
        "first_moment": centred(key_list[3], (D, COLS), 0.5, 3.0, ((0, 32),), jnp.float32),
        "second_moment": jnp.clip(jnp.exp(math.log(2.0) - 3.6888794 * jax.random.uniform(key_list[4], (D, COLS), jnp.float32) ** levels(key_list[4], (D, COLS), ((0, 32),), -0.2, 0.2)), 0.05, 2.0),
    }


beta_first = 0.9
beta_second = 0.95
learn_rate = 0.02
decay_rate = 0.1
epsilon = 1e-08

def apply_update(grads, master, first, second, total):
    rms_value = jnp.sqrt(total / (D * COLS))
    factor = 1.0 / jnp.maximum(rms_value, 1.0)
    clipped = grads * factor
    first_new = beta_first * first + (1.0 - beta_first) * clipped
    second_new = beta_second * second + (1.0 - beta_second) * clipped * clipped
    first_hat = first_new / (1.0 - beta_first ** STEP)
    second_hat = second_new / (1.0 - beta_second ** STEP)
    master_new = master - learn_rate * (first_hat / (jnp.sqrt(second_hat) + epsilon) + decay_rate * master)
    return (master_new, first_new, second_new)

def reference(tokens, cotangent, master, first_moment, second_moment):
    groups = N_REP * N_SHARD
    blocks = tokens.reshape(groups, TOK_DEV, D)
    cot_blocks = cotangent.reshape(groups, TOK_DEV, COLS)

    def accumulate(carry, pair):
        block, cot_block = pair
        partial_term = jnp.dot(block.astype(jnp.float32).T, cot_block.astype(jnp.float32), precision=lax.Precision.HIGHEST)
        rounded = lax.optimization_barrier(partial_term.astype(jnp.bfloat16)).astype(jnp.float32)
        return (carry + rounded, None)
    grads, _ = lax.scan(accumulate, jnp.zeros((D, COLS), jnp.float32), (blocks, cot_blocks))
    total = jnp.sum(grads * grads)
    master_new, first_new, second_new = apply_update(grads, master, first_moment, second_moment, total)
    weight = lax.optimization_barrier(master_new.astype(jnp.bfloat16)).astype(jnp.float32)

    def forward(block):
        return jnp.dot(block.astype(jnp.float32), weight, precision=lax.Precision.HIGHEST)
    outputs = lax.map(forward, blocks) * D ** (-0.5)
    activations = outputs.reshape(TOKENS, COLS).astype(jnp.bfloat16)
    return (master_new, first_new, second_new, activations)
```

```python
import jax
import jax.numpy as jnp
from jax import lax
from jax.sharding import Mesh, PartitionSpec as P

D = 12288
COLS = 256
STEP = 10

beta_first = 0.9
beta_second = 0.95
learn_rate = 0.02
decay_rate = 0.1
epsilon = 1e-08

NY, NC, NX, NZ = 4, 2, 4, 8
ROWS = D // (NX * NZ)
SIZE = {"y": NY, "core": NC, "x": NX, "z": NZ}
f32 = jnp.float32
bf16 = jnp.bfloat16


def apply_update(grads, master, first, second, total):
    rms_value = jnp.sqrt(total / (D * COLS))
    factor = 1.0 / jnp.maximum(rms_value, 1.0)
    clipped = grads * factor
    first_new = beta_first * first + (1.0 - beta_first) * clipped
    second_new = beta_second * second + (1.0 - beta_second) * clipped * clipped
    first_hat = first_new / (1.0 - beta_first**STEP)
    second_hat = second_new / (1.0 - beta_second**STEP)
    master_new = master - learn_rate * (
        first_hat / (jnp.sqrt(second_hat) + epsilon) + decay_rate * master
    )
    return (master_new, first_new, second_new)


def send(value, axis, step):
    n = SIZE[axis]
    return lax.ppermute(value, axis, [(i, (i + step) % n) for i in range(n)])


def order(n):
    return sorted(range(1, n), key=lambda d: -min(d, n - d))


def scatter_sum(value, axis, dim):
    n, me = SIZE[axis], lax.axis_index(axis)

    def entry(i):
        return lax.dynamic_index_in_dim(value, i, dim, keepdims=False)

    got = [send(entry((me + d) % n), axis, d) for d in order(n)]
    total = entry(me).astype(f32)
    for part in got:
        total = total + part.astype(f32)
    return total


def gather(value, axis, dim):
    n, me = SIZE[axis], lax.axis_index(axis)
    got = [(0, value)] + [(d, send(value, axis, d)) for d in order(n)]
    shape = value.shape[:dim] + (n,) + value.shape[dim:]
    out = jnp.zeros(shape, value.dtype)
    for d, part in got:
        out = lax.dynamic_update_slice_in_dim(
            out, jnp.expand_dims(part, dim), (me - d + n) % n, dim
        )
    return out


def all_sum(value, axis):
    total = value
    for d in order(SIZE[axis]):
        total = total + send(value, axis, d)
    return total


def cot_terms(cotangent, tokens):
    return lax.dot_general(
        cotangent, tokens, (((0,), (0,)), ((), ())), preferred_element_type=f32
    )


def body(tokens, cotangent, master, first_moment, second_moment):
    y, c = lax.axis_index("y"), lax.axis_index("core")
    half = COLS // 2
    own, other = c * half, (1 - c) * half
    cot_other = lax.dynamic_slice_in_dim(cotangent, other, half, 1)
    cot_own = lax.dynamic_slice_in_dim(cotangent, own, half, 1)
    arrived = send(cot_terms(cot_other, tokens).astype(bf16), "core", 1)
    chip = (cot_terms(cot_own, tokens) + arrived.astype(f32)).astype(bf16)
    chip = chip.reshape(NY, 2, 16, NX, NZ * ROWS)
    part_a, part_b = chip[:, 0], chip[:, 1]
    part_a = scatter_sum(part_a, "x", 2).astype(bf16)
    part_b = scatter_sum(part_b, "y", 0).astype(bf16)
    part_a = scatter_sum(part_a, "y", 0).astype(bf16)
    part_b = scatter_sum(part_b, "x", 1).astype(bf16)
    plane = jnp.concatenate([part_a, part_b]).reshape(32, NZ, ROWS)
    grads_piece = scatter_sum(plane, "z", 1)

    total = jnp.sum(grads_piece * grads_piece).reshape(1, 1)
    for axis in ("z", "x", "y", "core"):
        total = all_sum(total, axis)
    total = total[0, 0]

    col = c * half + y * 32

    def piece(state):
        return lax.dynamic_slice_in_dim(state, col, 32, 1).T

    weight_piece = apply_update(
        grads_piece, piece(master), piece(first_moment), piece(second_moment), total
    )[0].astype(bf16)

    plane = gather(weight_piece, "z", 1).reshape(2, 16, NZ * ROWS)
    part_a = gather(plane[0], "y", 0)
    part_b = gather(plane[1], "x", 1)
    part_a = gather(part_a, "x", 2)
    part_b = gather(part_b, "y", 0)
    weight_own = jnp.stack([part_a, part_b], 1).reshape(half, D)
    weight_other = send(weight_own, "core", 1)

    def product(weight):
        out = lax.dot_general(
            tokens, weight, (((1,), (1,)), ((), ())), preferred_element_type=f32
        )
        return (out * D ** (-0.5)).astype(bf16)

    act_own, act_other = product(weight_own), product(weight_other)
    activations = jnp.where(
        c == 0,
        jnp.concatenate([act_own, act_other], 1),
        jnp.concatenate([act_other, act_own], 1),
    )

    grads = gather(gather(grads_piece.astype(bf16), "y", 0), "core", 0)
    grads = grads.reshape(COLS, ROWS).T.astype(f32)
    master_new, first_new, second_new = apply_update(
        grads, master, first_moment, second_moment, total
    )
    return (master_new, first_new, second_new, activations)


def solution(mesh):
    names = ("y", "core", "x", "z")
    fine = Mesh(mesh.devices.reshape(NY, NC, NX, NZ), names)
    by_token, by_row = P(names, None), P(("x", "z"), None)
    return jax.shard_map(
        body,
        mesh=fine,
        in_specs=(by_token, by_token, by_row, by_row, by_row),
        out_specs=(by_row, by_row, by_row, by_token),
        check_vma=False,
    )
```

```python
import functools

import jax
import jax.numpy as jnp
from jax import lax
from jax.experimental import pallas as pl
from jax.experimental.pallas import tpu as pltpu
from jax.sharding import Mesh, PartitionSpec as P

STEP = 10

beta_first = 0.9
beta_second = 0.95
learn_rate = 0.02
decay_rate = 0.1
epsilon = 1e-08

NY, NC, NX, NZ = 4, 2, 4, 8
SIZE = {"y": NY, "core": NC, "x": NX, "z": NZ}
NAMES = ("y", "core", "x", "z")
f32 = jnp.float32
bf16 = jnp.bfloat16


def apply_update(grads, master, first, second, total, count):
    rms_value = jnp.sqrt(total / count)
    factor = 1.0 / jnp.maximum(rms_value, 1.0)
    clipped = grads * factor
    first_new = beta_first * first + (1.0 - beta_first) * clipped
    second_new = beta_second * second + (1.0 - beta_second) * clipped * clipped
    first_hat = first_new / (1.0 - beta_first**STEP)
    second_hat = second_new / (1.0 - beta_second**STEP)
    master_new = master - learn_rate * (
        first_hat / (jnp.sqrt(second_hat) + epsilon) + decay_rate * master
    )
    return (master_new, first_new, second_new)


def send(value, axis, step):
    n = SIZE[axis]
    return lax.ppermute(value, axis, [(i, (i + step) % n) for i in range(n)])


FAR_FIRST = (2, 1, 3)


def block_of(width):
    for size in (1024, 512, 384, 256, 128):
        if width % size == 0:
            return size
    return width


def partial_kernel(chunk_ref, cot_ref, tokens_ref, own_ref, other_ref):
    terms = jnp.dot(cot_ref[...], tokens_ref[...], preferred_element_type=f32).astype(bf16)
    half = terms.shape[0] // 2
    own_ref[...] = terms[:half]
    other_ref[...] = terms[half:]


def partial_terms(chunk, cot_rows, tokens):
    count, width = tokens.shape
    cols, chunk_width = cot_rows.shape[0], width // NX
    block = block_of(chunk_width)
    steps = chunk_width // block
    half = jax.ShapeDtypeStruct((cols // 2, chunk_width), bf16)
    out_spec = pl.BlockSpec((cols // 2, block), lambda i, c: (0, i))
    return pl.pallas_call(
        partial_kernel,
        grid_spec=pltpu.PrefetchScalarGridSpec(
            num_scalar_prefetch=1,
            grid=(steps,),
            in_specs=[
                pl.BlockSpec((cols, count), lambda i, c: (0, 0)),
                pl.BlockSpec((count, block), lambda i, c: (0, c[0] * steps + i)),
            ],
            out_specs=[out_spec, out_spec],
        ),
        out_shape=[half, half],
        cost_estimate=pl.CostEstimate(
            flops=2 * cols * count * chunk_width,
            bytes_accessed=2 * (count * chunk_width + cols * chunk_width + cols * count),
            transcendentals=0,
        ),
        name="partial_terms",
    )(chunk.reshape(1), cot_rows, tokens)


def forward_kernel(scale, chunk_ref, tokens_ref, weight_ref, out_ref, total):
    step = pl.program_id(0)

    @pl.when(step == 0)
    def _():
        total[...] = jnp.zeros_like(total)

    total[...] += lax.dot_general(
        tokens_ref[...], weight_ref[...], (((1,), (1,)), ((), ())), preferred_element_type=f32
    )

    @pl.when(step == pl.num_programs(0) - 1)
    def _():
        out_ref[...] = (total[...] * scale).astype(bf16)


def forward(x, tokens, weight):
    count, width = tokens.shape
    cols, chunk_width = weight.shape[0], width // NX
    block = block_of(chunk_width)
    steps = chunk_width // block
    return pl.pallas_call(
        functools.partial(forward_kernel, width ** (-0.5)),
        grid_spec=pltpu.PrefetchScalarGridSpec(
            num_scalar_prefetch=1,
            grid=(NX * steps,),
            in_specs=[
                pl.BlockSpec(
                    (count, block),
                    lambda i, c: (0, lax.rem(c[0] + NX - i // steps, NX) * steps + lax.rem(i, steps)),
                ),
                pl.BlockSpec((cols, block), lambda i, c: (0, i)),
            ],
            out_specs=pl.BlockSpec((count, cols), lambda i, c: (0, 0)),
            scratch_shapes=[pltpu.VMEM((count, cols), f32)],
        ),
        out_shape=jax.ShapeDtypeStruct((count, cols), bf16),
        cost_estimate=pl.CostEstimate(
            flops=2 * cols * count * width,
            bytes_accessed=2 * (count * width + cols * width + cols * count),
            transcendentals=0,
        ),
        name="forward",
    )(x.reshape(1), tokens, weight)


def rolled(value, y, back=False):
    shift = (NY - y) % NY if back else y
    wide = jnp.concatenate([value, value], -1)
    part = value.shape[-1] // NY
    return lax.dynamic_slice_in_dim(wide, shift * part, NY * part, value.ndim - 1)


def own_first(value, c, y, back=False):
    quarter = value.shape[1] // 4
    parts = [rolled(value[:, i * quarter : (i + 1) * quarter], y, back) for i in range(4)]
    lower, upper = jnp.concatenate(parts[:2], 1), jnp.concatenate(parts[2:], 1)
    return jnp.where(
        c == 0, jnp.concatenate([lower, upper], 1), jnp.concatenate([upper, lower], 1)
    )


def add(*parts):
    total = parts[0].astype(f32)
    for part in parts[1:]:
        total = total + part.astype(f32)
    return total


def body(tokens, cotangent, master, first_moment, second_moment):
    y, c, x = lax.axis_index("y"), lax.axis_index("core"), lax.axis_index("x")
    rows, cols = master.shape
    count = rows * NX * NZ * cols
    unit = cols // (NC * 2 * NY)
    quad = NY * unit
    span = rows * NZ

    cot_rows = own_first(cotangent, c, y).T
    chip = {}
    for d in (2, 1, 3, 0):
        own, other = partial_terms((x + d) % NX, cot_rows, tokens)
        chip[d] = add(own, send(other, "core", 1)).astype(bf16)
    got = [send(chip[d][:quad], "x", d) for d in FAR_FIRST]
    half_b = jnp.concatenate([chip[d][quad:] for d in range(NX)], 1)
    got_b = [send(half_b[d * unit : (d + 1) * unit], "y", d) for d in FAR_FIRST]
    half_a = add(chip[0][:quad], *got).astype(bf16)
    half_b = add(half_b[:unit], *got_b).astype(bf16)
    got = [send(half_a[d * unit : (d + 1) * unit], "y", d) for d in FAR_FIRST]
    got_b = [send(half_b[:, d * span : (d + 1) * span], "x", d) for d in FAR_FIRST]
    half_a = add(half_a[:unit], *got).astype(bf16)
    half_b = add(half_b[:, :span], *got_b).astype(bf16)
    plane = jnp.concatenate([half_a, half_b])
    planes = lax.all_to_all(plane, "z", 1, 0, tiled=True).reshape(NZ, 2 * unit, rows)
    piece = jnp.sum(planes.astype(f32), 0)

    square = jnp.sum(piece * piece).reshape(1, 1)
    squares = lax.all_to_all(
        jnp.broadcast_to(square, (NY * NC * NX * NZ, 1)), NAMES, 0, 0, tiled=True
    )
    total = jnp.sum(squares)
    piece = piece.astype(bf16)

    def state_piece(state):
        at = c * (cols // 2) + y * unit
        return jnp.concatenate(
            [lax.dynamic_slice_in_dim(state, at + h * quad, unit, 1) for h in range(2)], 1
        ).T

    states = [state_piece(state) for state in (master, first_moment, second_moment)]
    weight = apply_update(piece.astype(f32), *states, total, count)[0].astype(bf16)

    plane = lax.all_to_all(jnp.tile(weight, (NZ, 1)), "z", 0, 1, tiled=True)
    got = [plane[:unit]] + [send(plane[:unit], "y", d) for d in (1, 2, 3)]
    got_b = [plane[unit:]] + [send(plane[unit:], "x", d) for d in (1, 2, 3)]
    half_a = jnp.concatenate(got, 0)
    half_b = jnp.concatenate(got_b, 1)
    got = [half_a] + [send(half_a, "x", d) for d in (1, 2, 3)]
    got_b = [half_b] + [send(half_b, "y", d) for d in (1, 2, 3)]

    def whole(parts, parts_b):
        return [jnp.concatenate(parts, 1)] + parts_b

    other = [send(part, "core", 1) for part in got]
    other_b = [send(part, "core", 1) for part in got_b]
    weight = jnp.concatenate(whole(got, got_b) + whole(other, other_b), 0)
    out = forward(x, tokens, weight)
    pieces = [out[:, i * unit : (i + 1) * unit] for i in range(NC * 2 * NY)]
    out = jnp.concatenate(
        [pieces[q * NY + (NY - e) % NY] for q in range(NC * 2) for e in range(NY)], 1
    )
    activations = own_first(out, c, y, back=True)

    grads = lax.all_to_all(jnp.tile(piece, (NY * NC, 1)), ("core", "y"), 0, 0, tiled=True)
    grads = grads.reshape(NC, NY, 2, unit, rows).transpose(0, 2, 1, 3, 4).reshape(cols, rows)
    master_new, first_new, second_new = apply_update(
        grads.T.astype(f32), master, first_moment, second_moment, total, count
    )
    return (master_new, first_new, second_new, activations)


def solution(mesh):
    fine = Mesh(mesh.devices.reshape(NY, NC, NX, NZ), NAMES)
    by_token, by_row = P(NAMES, None), P(("x", "z"), None)
    return jax.shard_map(
        body,
        mesh=fine,
        in_specs=(by_token, by_token, by_row, by_row, by_row),
        out_specs=(by_row, by_row, by_row, by_token),
        check_vma=False,
    )
```

```python
import functools

import jax
import jax.numpy as jnp
from jax import lax
from jax.experimental import pallas as pl
from jax.experimental.pallas import tpu as pltpu
from jax.sharding import Mesh, PartitionSpec as P

STEP = 10

beta_first = 0.9
beta_second = 0.95
learn_rate = 0.02
decay_rate = 0.1
epsilon = 1e-08

NY, NC, NX, NZ = 4, 2, 4, 8
SIZE = {"y": NY, "core": NC, "x": NX, "z": NZ}
NAMES = ("y", "core", "x", "z")
f32 = jnp.float32
bf16 = jnp.bfloat16


def apply_update(grads, master, first, second, total, count):
    rms_value = jnp.sqrt(total / count)
    factor = 1.0 / jnp.maximum(rms_value, 1.0)
    clipped = grads * factor
    first_new = beta_first * first + (1.0 - beta_first) * clipped
    second_new = beta_second * second + (1.0 - beta_second) * clipped * clipped
    first_hat = first_new / (1.0 - beta_first**STEP)
    second_hat = second_new / (1.0 - beta_second**STEP)
    master_new = master - learn_rate * (
        first_hat / (jnp.sqrt(second_hat) + epsilon) + decay_rate * master
    )
    return (master_new, first_new, second_new)


def send(value, axis, step):
    n = SIZE[axis]
    return lax.ppermute(value, axis, [(i, (i + step) % n) for i in range(n)])


FAR_FIRST = (2, 1, 3)


def routed(value, step, first):
    pairs = []
    for y in range(NY):
        for c in range(NC):
            for x in range(NX):
                along_x = (c == 0) == first
                to_y, to_x = (y, (x + step) % NX) if along_x else ((y + step) % NY, x)
                pairs.append(((y * NC + c) * NX + x, (to_y * NC + c) * NX + to_x))
    return lax.ppermute(value, ("y", "core", "x"), pairs)


def block_of(width):
    for size in (1024, 512, 384, 256, 128):
        if width % size == 0:
            return size
    return width


def start_tokens(tokens_ref, held, sems, block, chunk_of):
    width = tokens_ref.shape[1]
    chunk = width // NX
    for i in range(width // block):
        d, at = i * block // chunk, i * block % chunk
        source = pl.multiple_of(chunk_of(d) * chunk + at, block)
        pltpu.make_async_copy(
            tokens_ref.at[:, pl.ds(source, block)],
            held.at[:, pl.ds(i * block, block)],
            sems.at[i],
        ).start()


def wait_tokens(tokens_ref, held, sems, block, i):
    at = pl.multiple_of(i * block, block)
    pltpu.make_async_copy(
        tokens_ref.at[:, pl.ds(0, block)], held.at[:, pl.ds(at, block)], sems.at[i]
    ).wait()
    return held[:, pl.ds(at, block)]


def partial_kernel(place_ref, cot_ref, tokens_ref, *refs):
    own, other = refs[:NX], refs[NX : 2 * NX]
    held, rows_t, rows, sems = refs[2 * NX :]
    y, c, x = place_ref[0], place_ref[1], place_ref[2]
    chunk = tokens_ref.shape[1] // NX
    half = rows.shape[0] // 2
    unit = half // NY
    block = block_of(chunk)
    start_tokens(tokens_ref, held, sems, block, lambda d: lax.rem(x + d, NX))
    rows_t[...] = cot_ref[...].astype(f32).T.astype(bf16)
    for k, core in enumerate((c, 1 - c)):
        for e in range(NY):
            at = pl.multiple_of(core * half + lax.rem(y + e, NY) * unit, unit)
            rows[pl.ds(k * half + e * unit, unit), :] = rows_t[pl.ds(at, unit), :]

    def run(by_x, by_y):
        steps = chunk // block
        first_x = by_x is own
        for d in range(NX):

            @pl.loop(0, steps)
            def _(j):
                part = wait_tokens(tokens_ref, held, sems, block, d * steps + j)
                lanes = pl.ds(pl.multiple_of(j * block, block), block)
                terms = jnp.dot(rows[...], part, preferred_element_type=f32).astype(bf16)
                mine, theirs = terms[:half], terms[half:]
                for_x, for_y = (mine, theirs) if first_x else (theirs, mine)
                by_x[d][:, lanes] = for_x
                for e in range(NY):
                    by_y[e][d * unit : (d + 1) * unit, lanes] = for_y[e * unit : (e + 1) * unit]

    @pl.when(c == 0)
    def _():
        run(own, other)

    @pl.when(c == 1)
    def _():
        run(other, own)


VMEM_LIMIT = 48 * 2**20


def partial_terms(place, cotangent, tokens):
    count, width = tokens.shape
    cols = cotangent.shape[1]
    block = block_of(width // NX)
    return pl.pallas_call(
        partial_kernel,
        in_specs=[
            pl.BlockSpec(memory_space=pltpu.SMEM),
            pl.BlockSpec(memory_space=pltpu.VMEM),
            pl.BlockSpec(memory_space=pl.ANY),
        ],
        out_specs=[pl.BlockSpec(memory_space=pltpu.VMEM)] * (2 * NX),
        out_shape=[jax.ShapeDtypeStruct((cols // 2, width // NX), bf16)] * (2 * NX),
        scratch_shapes=[
            pltpu.VMEM((count, width), bf16),
            pltpu.VMEM((cols, count), bf16),
            pltpu.VMEM((cols, count), bf16),
            pltpu.SemaphoreType.DMA((width // block,)),
        ],
        compiler_params=pltpu.CompilerParams(vmem_limit_bytes=VMEM_LIMIT),
        cost_estimate=pl.CostEstimate(
            flops=2 * cols * count * width,
            bytes_accessed=2 * (count * width + cols * width + cols * count),
            transcendentals=0,
        ),
        name="partial_terms",
    )(place, cotangent, tokens)


def forward_kernel(place_ref, tokens_ref, *refs):
    own, other = refs[:NX], refs[NX : 2 * NX]
    out_ref, held, weight, total, sems = refs[2 * NX :]
    y, c, x = place_ref[0], place_ref[1], place_ref[2]
    width = tokens_ref.shape[1]
    chunk = width // NX
    half = weight.shape[0] // 2
    unit = half // NY
    block = block_of(chunk)
    steps = chunk // block
    start_tokens(tokens_ref, held, sems, block, lambda d: lax.rem(x + NX - d, NX))

    def whole(by_x, by_y, d):
        for e in range(NY):
            at = pl.multiple_of(lax.rem(y + NY - e, NY) * unit, unit)
            weight[pl.ds(at, unit), :] = by_x[d][e * unit : (e + 1) * unit, :]
            weight[pl.ds(half + at, unit), :] = by_y[e][d * unit : (d + 1) * unit, :]

    for d in range(NX):

        @pl.when(c == 0)
        def _():
            whole(own, other, d)

        @pl.when(c == 1)
        def _():
            whole(other, own, d)

        @pl.loop(0, steps)
        def _(j):
            part = wait_tokens(tokens_ref, held, sems, block, d * steps + j)
            lanes = pl.ds(pl.multiple_of(j * block, block), block)
            terms = lax.dot_general(
                part, weight[:, lanes], (((1,), (1,)), ((), ())), preferred_element_type=f32
            )
            if d == 0:
                total[...] = jnp.where(j == 0, terms, total[...] + terms)
            else:
                total[...] += terms

    out_ref[...] = (total[...] * width ** (-0.5)).astype(bf16)


def forward(place, tokens, own, other):
    count, width = tokens.shape
    cols = 2 * own[0].shape[0]
    block = block_of(width // NX)
    return pl.pallas_call(
        forward_kernel,
        in_specs=[pl.BlockSpec(memory_space=pltpu.SMEM), pl.BlockSpec(memory_space=pl.ANY)]
        + [pl.BlockSpec(memory_space=pltpu.VMEM)] * (2 * NX),
        out_specs=pl.BlockSpec(memory_space=pltpu.VMEM),
        out_shape=jax.ShapeDtypeStruct((count, cols), bf16),
        scratch_shapes=[
            pltpu.VMEM((count, width), bf16),
            pltpu.VMEM((cols, width // NX), bf16),
            pltpu.VMEM((count, cols), f32),
            pltpu.SemaphoreType.DMA((width // block,)),
        ],
        compiler_params=pltpu.CompilerParams(vmem_limit_bytes=VMEM_LIMIT),
        cost_estimate=pl.CostEstimate(
            flops=2 * cols * count * width,
            bytes_accessed=2 * (count * width + cols * width + cols * count),
            transcendentals=0,
        ),
        name="forward",
    )(place, tokens, *own, *other)


def add(*parts):
    total = parts[0].astype(f32)
    for part in parts[1:]:
        total = total + part.astype(f32)
    return total


def body(tokens, cotangent, master, first_moment, second_moment):
    y, c, x = lax.axis_index("y"), lax.axis_index("core"), lax.axis_index("x")
    place = jnp.stack([y, c, x]).astype(jnp.int32)
    rows, cols = master.shape
    count = rows * NX * NZ * cols
    unit = cols // (NC * NY)

    terms = partial_terms(place, cotangent, tokens)
    own, other = terms[:NX], terms[NX:]
    chip = {}
    for d in (2, 1, 3, 0):
        chip[d] = add(own[d], send(other[d], "core", 1)).astype(bf16)
    got = [routed(chip[d], d, True) for d in FAR_FIRST]
    line = add(chip[0], *got).astype(bf16)
    got = [routed(line[d * unit : (d + 1) * unit], d, False) for d in FAR_FIRST]
    plane = add(line[:unit], *got).astype(bf16)
    planes = lax.all_to_all(plane, "z", 1, 0, tiled=True).reshape(NZ, unit, rows)
    piece = jnp.sum(planes.astype(f32), 0).astype(bf16)

    grads = lax.all_to_all(jnp.tile(piece, (NC * NY, 1)), ("core", "y"), 0, 0, tiled=True)
    grads = grads.astype(f32)
    square = jnp.sum(grads * grads).reshape(1, 1)
    squares = lax.all_to_all(
        jnp.broadcast_to(square, (NX * NZ, 1)), ("x", "z"), 0, 0, tiled=True
    )
    total = jnp.sum(squares)
    master_new, first_new, second_new = apply_update(
        grads.T, master, first_moment, second_moment, total, count
    )

    at = c * (cols // 2) + y * unit
    weight = lax.dynamic_slice_in_dim(master_new, at, unit, 1).T.astype(bf16)
    plane = lax.all_to_all(jnp.tile(weight, (NZ, 1)), "z", 0, 1, tiled=True)
    line = jnp.concatenate([plane] + [routed(plane, d, False) for d in (1, 2, 3)], 0)
    own = [line] + [routed(line, d, True) for d in (1, 2, 3)]
    other = [send(part, "core", 1) for part in own]
    activations = forward(place, tokens, own, other)
    return (master_new, first_new, second_new, activations)


def solution(mesh):
    fine = Mesh(mesh.devices.reshape(NY, NC, NX, NZ), NAMES)
    by_token, by_row = P(NAMES, None), P(("x", "z"), None)
    return jax.shard_map(
        body,
        mesh=fine,
        in_specs=(by_token, by_token, by_row, by_row, by_row),
        out_specs=(by_row, by_row, by_row, by_token),
        check_vma=False,
    )
```

```python
import functools

import jax
import jax.numpy as jnp
from jax import lax
from jax.experimental import pallas as pl
from jax.experimental.pallas import tpu as pltpu
from jax.sharding import Mesh, PartitionSpec as P

STEP = 10

beta_first = 0.9
beta_second = 0.95
learn_rate = 0.02
decay_rate = 0.1
epsilon = 1e-08

NY, NC, NX, NZ = 4, 2, 4, 8
SIZE = {"y": NY, "core": NC, "x": NX, "z": NZ}
NAMES = ("y", "core", "x", "z")
f32 = jnp.float32
bf16 = jnp.bfloat16


def apply_update(grads, master, first, second, total, count):
    rms_value = jnp.sqrt(total / count)
    factor = 1.0 / jnp.maximum(rms_value, 1.0)
    clipped = grads * factor
    first_new = beta_first * first + (1.0 - beta_first) * clipped
    second_new = beta_second * second + (1.0 - beta_second) * clipped * clipped
    first_hat = first_new / (1.0 - beta_first**STEP)
    second_hat = second_new / (1.0 - beta_second**STEP)
    master_new = master - learn_rate * (
        first_hat / (jnp.sqrt(second_hat) + epsilon) + decay_rate * master
    )
    return (master_new, first_new, second_new)


def send(value, axis, step):
    n = SIZE[axis]
    return lax.ppermute(value, axis, [(i, (i + step) % n) for i in range(n)])


FAR_FIRST = (2, 1, 3)


def routed(value, step, first):
    pairs = []
    for y in range(NY):
        for c in range(NC):
            for x in range(NX):
                along_x = (c == 0) == first
                to_y, to_x = (y, (x + step) % NX) if along_x else ((y + step) % NY, x)
                pairs.append(((y * NC + c) * NX + x, (to_y * NC + c) * NX + to_x))
    return lax.ppermute(value, ("y", "core", "x"), pairs)


VMEM_LIMIT = 24 * 2**20


def in_hbm(value):
    return pltpu.with_memory_space_constraint(value, pltpu.HBM)


def in_vmem(count):
    return [pl.BlockSpec(memory_space=pltpu.VMEM)] * count


def kernel_call(body, name, in_specs, out_shape, scratch=(), flops=0, moved=0):
    return pl.pallas_call(
        body,
        in_specs=in_specs,
        out_specs=in_vmem(len(out_shape)),
        out_shape=out_shape,
        scratch_shapes=list(scratch),
        compiler_params=pltpu.CompilerParams(vmem_limit_bytes=VMEM_LIMIT),
        cost_estimate=pl.CostEstimate(flops=flops, bytes_accessed=moved, transcendentals=0),
        name=name,
    )


def partial_kernel(place_ref, cot_ref, tokens_ref, *refs):
    own, other = refs[:NX], refs[NX : 2 * NX]
    held, cot, rows_t, rows, sems = refs[2 * NX :]
    y, c, x = place_ref[0], place_ref[1], place_ref[2]
    chunk = tokens_ref.shape[1] // NX
    half = rows.shape[0] // 2
    unit = half // NY
    cot_copy = pltpu.make_async_copy(cot_ref, cot, sems.at[NX])
    cot_copy.start()
    copies = []
    for d in range(NX):
        source = pl.multiple_of(lax.rem(x + d, NX) * chunk, chunk)
        copies.append(
            pltpu.make_async_copy(
                tokens_ref.at[:, pl.ds(source, chunk)],
                held.at[:, pl.ds(d * chunk, chunk)],
                sems.at[d],
            )
        )
        copies[-1].start()
    cot_copy.wait()
    rows_t[...] = cot[...].astype(f32).T.astype(bf16)
    for k, core in enumerate((c, 1 - c)):
        for e in range(NY):
            at = pl.multiple_of(core * half + lax.rem(y + e, NY) * unit, unit)
            rows[pl.ds(k * half + e * unit, unit), :] = rows_t[pl.ds(at, unit), :]

    for d in range(NX):
        copies[d].wait()

        def run(by_x, by_y):
            terms = jnp.dot(
                rows[...], held[:, d * chunk : (d + 1) * chunk], preferred_element_type=f32
            ).astype(bf16)
            mine, theirs = terms[:half], terms[half:]
            for_x, for_y = (mine, theirs) if by_x is own else (theirs, mine)
            by_x[d][...] = for_x
            for e in range(NY):
                by_y[e][d * unit : (d + 1) * unit, :] = for_y[e * unit : (e + 1) * unit]

        @pl.when(c == 0)
        def _():
            run(own, other)

        @pl.when(c == 1)
        def _():
            run(other, own)


def partial_terms(place, cotangent, tokens):
    count, width = tokens.shape
    cols = cotangent.shape[1]
    part = jax.ShapeDtypeStruct((cols // 2, width // NX), bf16)
    out = kernel_call(
        partial_kernel,
        "partial_terms",
        [
            pl.BlockSpec(memory_space=pltpu.SMEM),
            pl.BlockSpec(memory_space=pltpu.HBM),
            pl.BlockSpec(memory_space=pltpu.HBM),
        ],
        [part] * (2 * NX) + [jax.ShapeDtypeStruct((count, width), bf16)],
        [
            pltpu.VMEM((count, cols), bf16),
            pltpu.VMEM((cols, count), bf16),
            pltpu.VMEM((cols, count), bf16),
            pltpu.SemaphoreType.DMA((NX + 1,)),
        ],
        2 * cols * count * width,
        2 * (count * width + cols * width + cols * count),
    )(place, in_hbm(cotangent), in_hbm(tokens))
    return out[:NX], out[NX : 2 * NX], out[2 * NX]


def forward_kernel(place_ref, held, *refs):
    own, other = refs[:NX], refs[NX : 2 * NX]
    out_ref, weight, total = refs[2 * NX :]
    y, c = place_ref[0], place_ref[1]
    width = held.shape[1]
    chunk = width // NX
    half = weight.shape[1] // 2
    unit = half // NY

    def run(by_x, by_y):
        for d in range(NX):
            for e in range(NY):
                at = pl.multiple_of(lax.rem(y + NY - e, NY) * unit, unit)
                weight[d, pl.ds(at, unit), :] = by_x[d][e * unit : (e + 1) * unit, :]
                weight[d, pl.ds(half + at, unit), :] = by_y[e][d * unit : (d + 1) * unit, :]
            back = (NX - d) % NX
            terms = lax.dot_general(
                held[:, back * chunk : (back + 1) * chunk],
                weight[d],
                (((1,), (1,)), ((), ())),
                preferred_element_type=f32,
            )
            if d == 0:
                total[...] = terms
            else:
                total[...] += terms

    @pl.when(c == 0)
    def _():
        run(own, other)

    @pl.when(c == 1)
    def _():
        run(other, own)

    out_ref[...] = (total[...] * width ** (-0.5)).astype(bf16)


def forward(place, held, own, other):
    count, width = held.shape
    cols = 2 * own[0].shape[0]
    return kernel_call(
        forward_kernel,
        "forward",
        [pl.BlockSpec(memory_space=pltpu.SMEM)] + in_vmem(1 + 2 * NX),
        [jax.ShapeDtypeStruct((count, cols), bf16)],
        [pltpu.VMEM((NX, cols, width // NX), bf16), pltpu.VMEM((count, cols), f32)],
        2 * cols * count * width,
        2 * (count * width + cols * width + cols * count),
    )(place, held, *own, *other)[0]


def plane_kernel(planes_ref, piece_ref, squares_ref):
    unit = piece_ref.shape[0]
    total = planes_ref[:unit].astype(f32)
    for z in range(1, NZ):
        total += planes_ref[z * unit : (z + 1) * unit].astype(f32)
    piece_ref[...] = total.astype(bf16)
    squares_ref[...] = jnp.broadcast_to(jnp.sum(total * total), squares_ref.shape)


def plane_sum(planes):
    unit, rows = planes.shape[0] // NZ, planes.shape[1]
    everyone = NY * NC * NX * NZ
    return kernel_call(
        plane_kernel,
        "plane_sum",
        in_vmem(1),
        [jax.ShapeDtypeStruct((unit, rows), bf16), jax.ShapeDtypeStruct((everyone, 128), f32)],
    )(planes)


def weight_kernel(count, place_ref, piece_ref, squares_ref, *refs):
    states, (out_ref, wide, turned) = refs[:3], refs[3:]
    y, c = place_ref[0], place_ref[1]
    unit, rows = piece_ref.shape
    half = wide.shape[1]
    at = pl.multiple_of(y * unit, unit)
    lanes = pl.ds(pl.multiple_of(c * half, half), half)
    total = jnp.sum(squares_ref[:, :1])
    turned[...] = jnp.zeros_like(turned)
    turned[pl.ds(at, unit), :] = piece_ref[...].astype(f32)
    wide[...] = turned[...].T
    new = apply_update(wide[...], *[state[:, lanes] for state in states], total, count)[0]
    turned[...] = new.T
    mine = turned[pl.ds(at, unit), :].astype(bf16)
    for z in range(NZ):
        out_ref[z * unit : (z + 1) * unit, :] = mine


def weight_piece(place, piece, squares, states, count):
    unit, rows = piece.shape
    half = states[0].shape[1] // 2
    return kernel_call(
        functools.partial(weight_kernel, count),
        "weight_piece",
        [pl.BlockSpec(memory_space=pltpu.SMEM)] + in_vmem(2 + len(states)),
        [jax.ShapeDtypeStruct((NZ * unit, rows), bf16)],
        [pltpu.VMEM((rows, half), f32), pltpu.VMEM((half, rows), f32)],
    )(place, piece, squares, *states)[0]


def spread_kernel(piece_ref, after_ref, out_ref):
    del after_ref
    unit = piece_ref.shape[0]
    for i in range(out_ref.shape[0] // unit):
        out_ref[i * unit : (i + 1) * unit, :] = piece_ref[...]


def spread(piece, copies, after):
    unit, rows = piece.shape
    return kernel_call(
        spread_kernel,
        "spread",
        in_vmem(1) + [pl.BlockSpec(memory_space=pl.ANY)],
        [jax.ShapeDtypeStruct((copies * unit, rows), bf16)],
    )(piece, after)[0]


def update_kernel(count, grads_ref, squares_ref, *refs):
    total = jnp.sum(squares_ref[:, :1])
    new = apply_update(grads_ref[...].astype(f32).T, *[ref[...] for ref in refs[:3]], total, count)
    for ref, value in zip(refs[3:], new):
        ref[...] = value


def update(grads, squares, states, count):
    return kernel_call(
        functools.partial(update_kernel, count),
        "update",
        in_vmem(2 + len(states)),
        [jax.ShapeDtypeStruct(states[0].shape, f32)] * 3,
    )(grads, squares, *states)


def add(*parts):
    total = parts[0].astype(f32)
    for part in parts[1:]:
        total = total + part.astype(f32)
    return total


def body(tokens, cotangent, master, first_moment, second_moment):
    y, c, x = lax.axis_index("y"), lax.axis_index("core"), lax.axis_index("x")
    place = jnp.stack([y, c, x]).astype(jnp.int32)
    states = (master, first_moment, second_moment)
    rows, cols = master.shape
    count = rows * NX * NZ * cols
    unit = cols // (NC * NY)

    own, other, held = partial_terms(place, cotangent, tokens)
    chip = {}
    for d in (2, 1, 3, 0):
        chip[d] = add(own[d], send(other[d], "core", 1)).astype(bf16)
    got = [routed(chip[d], d, True) for d in FAR_FIRST]
    line = add(chip[0], *got).astype(bf16)
    got = [routed(line[d * unit : (d + 1) * unit], d, False) for d in FAR_FIRST]
    plane = add(line[:unit], *got).astype(bf16)
    planes = lax.all_to_all(plane, "z", 1, 0, tiled=True)
    piece, squares = plane_sum(planes)
    squares = lax.all_to_all(squares, NAMES, 0, 0, tiled=True)

    weight = weight_piece(place, piece, squares, states, count)
    plane = lax.all_to_all(weight, "z", 0, 1, tiled=True)
    line = jnp.concatenate([plane] + [routed(plane, d, False) for d in (1, 2, 3)], 0)
    own = [line] + [routed(line, d, True) for d in (1, 2, 3)]
    other = [send(part, "core", 1) for part in own]

    grads = lax.all_to_all(spread(piece, NC * NY, other[0]), ("core", "y"), 0, 0, tiled=True)
    master_new, first_new, second_new = update(grads, squares, states, count)
    activations = forward(place, held, own, other)
    return (master_new, first_new, second_new, activations)


def solution(mesh):
    fine = Mesh(mesh.devices.reshape(NY, NC, NX, NZ), NAMES)
    by_token, by_row = P(NAMES, None), P(("x", "z"), None)
    return jax.shard_map(
        body,
        mesh=fine,
        in_specs=(by_token, by_token, by_row, by_row, by_row),
        out_specs=(by_row, by_row, by_row, by_token),
        check_vma=False,
    )
```

```python
import functools

import jax
import jax.numpy as jnp
from jax import lax
from jax.experimental import pallas as pl
from jax.experimental.pallas import tpu as pltpu
from jax.sharding import Mesh, PartitionSpec as P

STEP = 10

beta_first = 0.9
beta_second = 0.95
learn_rate = 0.02
decay_rate = 0.1
epsilon = 1e-08

NY, NC, NX, NZ = 4, 2, 4, 8
SIZE = {"y": NY, "core": NC, "x": NX, "z": NZ}
NAMES = ("y", "core", "x", "z")
f32 = jnp.float32
bf16 = jnp.bfloat16


def apply_update(grads, master, first, second, total, count):
    rms_value = jnp.sqrt(total / count)
    factor = 1.0 / jnp.maximum(rms_value, 1.0)
    clipped = grads * factor
    first_new = beta_first * first + (1.0 - beta_first) * clipped
    second_new = beta_second * second + (1.0 - beta_second) * clipped * clipped
    first_hat = first_new / (1.0 - beta_first**STEP)
    second_hat = second_new / (1.0 - beta_second**STEP)
    master_new = master - learn_rate * (
        first_hat / (jnp.sqrt(second_hat) + epsilon) + decay_rate * master
    )
    return (master_new, first_new, second_new)


def send(value, axis, step):
    n = SIZE[axis]
    return lax.ppermute(value, axis, [(i, (i + step) % n) for i in range(n)])


FAR_FIRST = (2, 1, 3)


def routed(value, step, first):
    pairs = []
    for y in range(NY):
        for c in range(NC):
            for x in range(NX):
                along_x = (c == 0) == first
                to_y, to_x = (y, (x + step) % NX) if along_x else ((y + step) % NY, x)
                pairs.append(((y * NC + c) * NX + x, (to_y * NC + c) * NX + to_x))
    return lax.ppermute(value, ("y", "core", "x"), pairs)


VMEM_LIMIT = 24 * 2**20


def in_hbm(value):
    return pltpu.with_memory_space_constraint(value, pltpu.HBM)


def in_vmem(count):
    return [pl.BlockSpec(memory_space=pltpu.VMEM)] * count


def kernel_call(body, name, in_specs, out_shape, scratch=(), flops=0, moved=0):
    return pl.pallas_call(
        body,
        in_specs=in_specs,
        out_specs=in_vmem(len(out_shape)),
        out_shape=out_shape,
        scratch_shapes=list(scratch),
        compiler_params=pltpu.CompilerParams(vmem_limit_bytes=VMEM_LIMIT),
        cost_estimate=pl.CostEstimate(flops=flops, bytes_accessed=moved, transcendentals=0),
        name=name,
    )


def partial_kernel(place_ref, cot_ref, tokens_ref, *refs):
    own, other = refs[:NX], refs[NX : 2 * NX]
    held, cot, rows_t, rows, sems = refs[2 * NX :]
    y, c, x = place_ref[0], place_ref[1], place_ref[2]
    chunk = tokens_ref.shape[1] // NX
    half = rows.shape[0] // 2
    unit = half // NY
    cot_copy = pltpu.make_async_copy(cot_ref, cot, sems.at[NX])
    cot_copy.start()
    copies = []
    for d in range(NX):
        source = pl.multiple_of(lax.rem(x + d, NX) * chunk, chunk)
        copies.append(
            pltpu.make_async_copy(
                tokens_ref.at[:, pl.ds(source, chunk)],
                held.at[:, pl.ds(d * chunk, chunk)],
                sems.at[d],
            )
        )
        copies[-1].start()
    cot_copy.wait()
    rows_t[...] = cot[...].astype(f32).T.astype(bf16)
    for k, core in enumerate((c, 1 - c)):
        for e in range(NY):
            at = pl.multiple_of(core * half + lax.rem(y + e, NY) * unit, unit)
            rows[pl.ds(k * half + e * unit, unit), :] = rows_t[pl.ds(at, unit), :]

    for d in range(NX):
        copies[d].wait()

        def run(by_x, by_y):
            terms = jnp.dot(
                rows[...], held[:, d * chunk : (d + 1) * chunk], preferred_element_type=f32
            ).astype(bf16)
            mine, theirs = terms[:half], terms[half:]
            for_x, for_y = (mine, theirs) if by_x is own else (theirs, mine)
            by_x[d][...] = for_x
            for e in range(NY):
                by_y[e][d * unit : (d + 1) * unit, :] = for_y[e * unit : (e + 1) * unit]

        @pl.when(c == 0)
        def _():
            run(own, other)

        @pl.when(c == 1)
        def _():
            run(other, own)


def partial_terms(place, cotangent, tokens):
    count, width = tokens.shape
    cols = cotangent.shape[1]
    part = jax.ShapeDtypeStruct((cols // 2, width // NX), bf16)
    out = kernel_call(
        partial_kernel,
        "partial_terms",
        [
            pl.BlockSpec(memory_space=pltpu.SMEM),
            pl.BlockSpec(memory_space=pltpu.HBM),
            pl.BlockSpec(memory_space=pltpu.HBM),
        ],
        [part] * (2 * NX) + [jax.ShapeDtypeStruct((count, width), bf16)],
        [
            pltpu.VMEM((count, cols), bf16),
            pltpu.VMEM((cols, count), bf16),
            pltpu.VMEM((cols, count), bf16),
            pltpu.SemaphoreType.DMA((NX + 1,)),
        ],
        2 * cols * count * width,
        2 * (count * width + cols * width + cols * count),
    )(place, in_hbm(cotangent), in_hbm(tokens))
    return out[:NX], out[NX : 2 * NX], out[2 * NX]


def forward_kernel(place_ref, held, *refs):
    own, other = refs[:NX], refs[NX : 2 * NX]
    out_ref, weight, total = refs[2 * NX :]
    y, c = place_ref[0], place_ref[1]
    width = held.shape[1]
    chunk = width // NX
    half = weight.shape[1] // 2
    unit = half // NY

    def run(by_x, by_y):
        for d in range(NX):
            for e in range(NY):
                at = pl.multiple_of(lax.rem(y + NY - e, NY) * unit, unit)
                weight[d, pl.ds(at, unit), :] = by_x[d][e * unit : (e + 1) * unit, :]
                weight[d, pl.ds(half + at, unit), :] = by_y[e][d * unit : (d + 1) * unit, :]
            back = (NX - d) % NX
            terms = lax.dot_general(
                held[:, back * chunk : (back + 1) * chunk],
                weight[d],
                (((1,), (1,)), ((), ())),
                preferred_element_type=f32,
            )
            if d == 0:
                total[...] = terms
            else:
                total[...] += terms

    @pl.when(c == 0)
    def _():
        run(own, other)

    @pl.when(c == 1)
    def _():
        run(other, own)

    out_ref[...] = (total[...] * width ** (-0.5)).astype(bf16)


def forward(place, held, own, other):
    count, width = held.shape
    cols = 2 * own[0].shape[0]
    return kernel_call(
        forward_kernel,
        "forward",
        [pl.BlockSpec(memory_space=pltpu.SMEM)] + in_vmem(1 + 2 * NX),
        [jax.ShapeDtypeStruct((count, cols), bf16)],
        [pltpu.VMEM((NX, cols, width // NX), bf16), pltpu.VMEM((count, cols), f32)],
        2 * cols * count * width,
        2 * (count * width + cols * width + cols * count),
    )(place, held, *own, *other)[0]


def plane_kernel(planes_ref, piece_ref, squares_ref):
    unit = piece_ref.shape[0]
    total = planes_ref[:unit].astype(f32)
    for z in range(1, NZ):
        total += planes_ref[z * unit : (z + 1) * unit].astype(f32)
    piece_ref[...] = total.astype(bf16)
    squares_ref[...] = jnp.broadcast_to(jnp.sum(total * total), squares_ref.shape)


def plane_sum(planes):
    unit, rows = planes.shape[0] // NZ, planes.shape[1]
    everyone = NY * NC * NX * NZ
    return kernel_call(
        plane_kernel,
        "plane_sum",
        in_vmem(1),
        [jax.ShapeDtypeStruct((unit, rows), bf16), jax.ShapeDtypeStruct((everyone, 128), f32)],
    )(planes)


def weight_kernel(count, place_ref, piece_ref, squares_ref, *refs):
    states, (out_ref, wide, turned) = refs[:3], refs[3:]
    y, c = place_ref[0], place_ref[1]
    unit, rows = piece_ref.shape
    half = wide.shape[1]
    at = pl.multiple_of(y * unit, unit)
    lanes = pl.ds(pl.multiple_of(c * half, half), half)
    total = jnp.sum(squares_ref[:, :1])
    turned[...] = jnp.zeros_like(turned)
    turned[pl.ds(at, unit), :] = piece_ref[...].astype(f32)
    wide[...] = turned[...].T
    new = apply_update(wide[...], *[state[:, lanes] for state in states], total, count)[0]
    turned[...] = new.T
    mine = turned[pl.ds(at, unit), :].astype(bf16)
    for z in range(NZ):
        out_ref[z * unit : (z + 1) * unit, :] = mine


def weight_piece(place, piece, squares, states, count):
    unit, rows = piece.shape
    half = states[0].shape[1] // 2
    return kernel_call(
        functools.partial(weight_kernel, count),
        "weight_piece",
        [pl.BlockSpec(memory_space=pltpu.SMEM)] + in_vmem(2 + len(states)),
        [jax.ShapeDtypeStruct((NZ * unit, rows), bf16)],
        [pltpu.VMEM((rows, half), f32), pltpu.VMEM((half, rows), f32)],
    )(place, piece, squares, *states)[0]


def spread_kernel(piece_ref, after_ref, out_ref):
    del after_ref
    unit = piece_ref.shape[0]
    for i in range(out_ref.shape[0] // unit):
        out_ref[i * unit : (i + 1) * unit, :] = piece_ref[...]


def spread(piece, copies, after):
    unit, rows = piece.shape
    return kernel_call(
        spread_kernel,
        "spread",
        in_vmem(1) + [pl.BlockSpec(memory_space=pl.ANY)],
        [jax.ShapeDtypeStruct((copies * unit, rows), bf16)],
    )(piece, after)[0]


def tie_kernel(value_ref, after_ref, out_ref):
    pass


def tie(value, after):
    return pl.pallas_call(
        tie_kernel,
        in_specs=[pl.BlockSpec(memory_space=pl.ANY)] * 2,
        out_specs=pl.BlockSpec(memory_space=pl.ANY),
        out_shape=jax.ShapeDtypeStruct(value.shape, value.dtype),
        input_output_aliases={0: 0},
        name="tie",
    )(value, after)


def update_kernel(count, grads_ref, squares_ref, *refs):
    total = jnp.sum(squares_ref[:, :1])
    new = apply_update(grads_ref[...].astype(f32).T, *[ref[...] for ref in refs[:3]], total, count)
    for ref, value in zip(refs[3:], new):
        ref[...] = value


def update(grads, squares, states, count):
    return kernel_call(
        functools.partial(update_kernel, count),
        "update",
        in_vmem(2 + len(states)),
        [jax.ShapeDtypeStruct(states[0].shape, f32)] * 3,
    )(grads, squares, *states)


def add(*parts):
    total = parts[0].astype(f32)
    for part in parts[1:]:
        total = total + part.astype(f32)
    return total


def body(tokens, cotangent, master, first_moment, second_moment):
    y, c, x = lax.axis_index("y"), lax.axis_index("core"), lax.axis_index("x")
    place = jnp.stack([y, c, x]).astype(jnp.int32)
    states = (master, first_moment, second_moment)
    rows, cols = master.shape
    count = rows * NX * NZ * cols
    unit = cols // (NC * NY)

    own, other, held = partial_terms(place, cotangent, tokens)
    chip = {}
    for d in (2, 1, 3, 0):
        chip[d] = add(own[d], send(other[d], "core", 1)).astype(bf16)
    got = [routed(chip[d], d, True) for d in FAR_FIRST]
    line = add(chip[0], *got).astype(bf16)
    got = [routed(line[d * unit : (d + 1) * unit], d, False) for d in FAR_FIRST]
    plane = add(line[:unit], *got).astype(bf16)
    planes = lax.all_to_all(plane, "z", 1, 0, tiled=True)
    piece, squares = plane_sum(planes)
    squares = lax.all_to_all(squares, NAMES, 0, 0, tiled=True)

    weight = weight_piece(place, piece, squares, states, count)
    plane = lax.all_to_all(weight, "z", 0, 1, tiled=True)
    line = jnp.concatenate([plane] + [routed(plane, d, False) for d in (1, 2, 3)], 0)
    own = [line] + [routed(line, d, True) for d in (1, 2, 3)]
    grads = lax.all_to_all(spread(piece, NC * NY, own[3]), ("core", "y"), 0, 0, tiled=True)
    master_new, first_new, second_new = update(grads, squares, states, count)
    own[1] = tie(own[1], master_new)
    other = [send(part, "core", 1) for part in own]
    activations = forward(place, held, own, other)
    return (master_new, first_new, second_new, activations)


def solution(mesh):
    fine = Mesh(mesh.devices.reshape(NY, NC, NX, NZ), NAMES)
    by_token, by_row = P(NAMES, None), P(("x", "z"), None)
    return jax.shard_map(
        body,
        mesh=fine,
        in_specs=(by_token, by_token, by_row, by_row, by_row),
        out_specs=(by_row, by_row, by_row, by_token),
        check_vma=False,
    )
```

```python
import functools

import jax
import jax.numpy as jnp
from jax import lax
from jax.experimental import pallas as pl
from jax.experimental.pallas import tpu as pltpu
from jax.sharding import Mesh, PartitionSpec as P

STEP = 10

beta_first = 0.9
beta_second = 0.95
learn_rate = 0.02
decay_rate = 0.1
epsilon = 1e-08

NY, NC, NX, NZ = 4, 2, 4, 8
SIZE = {"y": NY, "core": NC, "x": NX, "z": NZ}
NAMES = ("y", "core", "x", "z")
f32 = jnp.float32
bf16 = jnp.bfloat16


def apply_update(grads, master, first, second, total, count):
    rms_value = jnp.sqrt(total / count)
    factor = 1.0 / jnp.maximum(rms_value, 1.0)
    clipped = grads * factor
    first_new = beta_first * first + (1.0 - beta_first) * clipped
    second_new = beta_second * second + (1.0 - beta_second) * clipped * clipped
    first_hat = first_new / (1.0 - beta_first**STEP)
    second_hat = second_new / (1.0 - beta_second**STEP)
    master_new = master - learn_rate * (
        first_hat / (jnp.sqrt(second_hat) + epsilon) + decay_rate * master
    )
    return (master_new, first_new, second_new)


def send(value, axis, step):
    n = SIZE[axis]
    return lax.ppermute(value, axis, [(i, (i + step) % n) for i in range(n)])


FAR_FIRST = (2, 1, 3)


def routed(value, step, first):
    pairs = []
    for y in range(NY):
        for c in range(NC):
            for x in range(NX):
                along_x = (c == 0) == first
                to_y, to_x = (y, (x + step) % NX) if along_x else ((y + step) % NY, x)
                pairs.append(((y * NC + c) * NX + x, (to_y * NC + c) * NX + to_x))
    return lax.ppermute(value, ("y", "core", "x"), pairs)


MIB = 2**20


def in_hbm(value):
    return pltpu.with_memory_space_constraint(value, pltpu.HBM)


def in_vmem(count):
    return [pl.BlockSpec(memory_space=pltpu.VMEM)] * count


def kernel_call(body, name, in_specs, out_shape, scratch=(), flops=0, moved=0, vmem=8 * MIB):
    return pl.pallas_call(
        body,
        in_specs=in_specs,
        out_specs=in_vmem(len(out_shape)),
        out_shape=out_shape,
        scratch_shapes=list(scratch),
        compiler_params=pltpu.CompilerParams(vmem_limit_bytes=vmem),
        cost_estimate=pl.CostEstimate(flops=flops, bytes_accessed=moved, transcendentals=0),
        name=name,
    )


def partial_kernel(place_ref, cot_ref, tokens_ref, *refs):
    own, other = refs[:NX], refs[NX : 2 * NX]
    held, cot, rows_t, rows, sems = refs[2 * NX :]
    y, c, x = place_ref[0], place_ref[1], place_ref[2]
    chunk = tokens_ref.shape[1] // NX
    half = rows.shape[0] // 2
    unit = half // NY
    cot_copy = pltpu.make_async_copy(cot_ref, cot, sems.at[NX])
    cot_copy.start()
    copies = []
    for d in range(NX):
        source = pl.multiple_of(lax.rem(x + d, NX) * chunk, chunk)
        copies.append(
            pltpu.make_async_copy(
                tokens_ref.at[:, pl.ds(source, chunk)],
                held.at[:, pl.ds(d * chunk, chunk)],
                sems.at[d],
            )
        )
        copies[-1].start()
    cot_copy.wait()
    rows_t[...] = cot[...].astype(f32).T.astype(bf16)
    for k, core in enumerate((c, 1 - c)):
        for e in range(NY):
            at = pl.multiple_of(core * half + lax.rem(y + e, NY) * unit, unit)
            rows[pl.ds(k * half + e * unit, unit), :] = rows_t[pl.ds(at, unit), :]

    for d in range(NX):
        copies[d].wait()

        def run(by_x, by_y):
            terms = jnp.dot(
                rows[...], held[:, d * chunk : (d + 1) * chunk], preferred_element_type=f32
            ).astype(bf16)
            mine, theirs = terms[:half], terms[half:]
            for_x, for_y = (mine, theirs) if by_x is own else (theirs, mine)
            by_x[d][...] = for_x
            for e in range(NY):
                by_y[e][d * unit : (d + 1) * unit, :] = for_y[e * unit : (e + 1) * unit]

        @pl.when(c == 0)
        def _():
            run(own, other)

        @pl.when(c == 1)
        def _():
            run(other, own)


def partial_terms(place, cotangent, tokens):
    count, width = tokens.shape
    cols = cotangent.shape[1]
    part = jax.ShapeDtypeStruct((cols // 2, width // NX), bf16)
    out = kernel_call(
        partial_kernel,
        "partial_terms",
        [
            pl.BlockSpec(memory_space=pltpu.SMEM),
            pl.BlockSpec(memory_space=pltpu.HBM),
            pl.BlockSpec(memory_space=pltpu.HBM),
        ],
        [part] * (2 * NX) + [jax.ShapeDtypeStruct((count, width), bf16)],
        [
            pltpu.VMEM((count, cols), bf16),
            pltpu.VMEM((cols, count), bf16),
            pltpu.VMEM((cols, count), bf16),
            pltpu.SemaphoreType.DMA((NX + 1,)),
        ],
        2 * cols * count * width,
        2 * (count * width + cols * width + cols * count),
        16 * MIB,
    )(place, in_hbm(cotangent), in_hbm(tokens))
    return out[:NX], out[NX : 2 * NX], out[2 * NX]


def forward_kernel(place_ref, held, *refs):
    own, other = refs[:NX], refs[NX : 2 * NX]
    out_ref, weight, total = refs[2 * NX :]
    y, c = place_ref[0], place_ref[1]
    width = held.shape[1]
    chunk = width // NX
    half = weight.shape[1] // 2
    unit = half // NY

    def run(by_x, by_y):
        for d in range(NX):
            for e in range(NY):
                at = pl.multiple_of(lax.rem(y + NY - e, NY) * unit, unit)
                weight[d, pl.ds(at, unit), :] = by_x[d][e * unit : (e + 1) * unit, :]
                weight[d, pl.ds(half + at, unit), :] = by_y[e][d * unit : (d + 1) * unit, :]
            back = (NX - d) % NX
            terms = lax.dot_general(
                held[:, back * chunk : (back + 1) * chunk],
                weight[d],
                (((1,), (1,)), ((), ())),
                preferred_element_type=f32,
            )
            if d == 0:
                total[...] = terms
            else:
                total[...] += terms

    @pl.when(c == 0)
    def _():
        run(own, other)

    @pl.when(c == 1)
    def _():
        run(other, own)

    out_ref[...] = (total[...] * width ** (-0.5)).astype(bf16)


def forward(place, held, own, other):
    count, width = held.shape
    cols = 2 * own[0].shape[0]
    return kernel_call(
        forward_kernel,
        "forward",
        [pl.BlockSpec(memory_space=pltpu.SMEM)] + in_vmem(1 + 2 * NX),
        [jax.ShapeDtypeStruct((count, cols), bf16)],
        [pltpu.VMEM((NX, cols, width // NX), bf16), pltpu.VMEM((count, cols), f32)],
        2 * cols * count * width,
        2 * (count * width + cols * width + cols * count),
        16 * MIB,
    )(place, held, *own, *other)[0]


def plane_kernel(planes_ref, piece_ref, squares_ref):
    unit = piece_ref.shape[0]
    total = planes_ref[:unit].astype(f32)
    for z in range(1, NZ):
        total += planes_ref[z * unit : (z + 1) * unit].astype(f32)
    piece_ref[...] = total.astype(bf16)
    squares_ref[...] = jnp.broadcast_to(jnp.sum(total * total), squares_ref.shape)


def plane_sum(planes):
    unit, rows = planes.shape[0] // NZ, planes.shape[1]
    everyone = NY * NC * NX * NZ
    return kernel_call(
        plane_kernel,
        "plane_sum",
        in_vmem(1),
        [jax.ShapeDtypeStruct((unit, rows), bf16), jax.ShapeDtypeStruct((everyone, 128), f32)],
    )(planes)


def weight_kernel(count, place_ref, piece_ref, squares_ref, *refs):
    states, (out_ref, wide, turned) = refs[:3], refs[4:]
    y, c = place_ref[0], place_ref[1]
    unit, rows = piece_ref.shape
    half = wide.shape[1]
    at = pl.multiple_of(y * unit, unit)
    lanes = pl.ds(pl.multiple_of(c * half, half), half)
    total = jnp.sum(squares_ref[:, :1])
    turned[...] = jnp.zeros_like(turned)
    turned[pl.ds(at, unit), :] = piece_ref[...].astype(f32)
    wide[...] = turned[...].T
    new = apply_update(wide[...], *[state[:, lanes] for state in states], total, count)[0]
    turned[...] = new.T
    mine = turned[pl.ds(at, unit), :].astype(bf16)
    for z in range(NZ):
        out_ref[z * unit : (z + 1) * unit, :] = mine


def weight_piece(place, piece, squares, states, after, count):
    unit, rows = piece.shape
    half = states[0].shape[1] // 2
    return kernel_call(
        functools.partial(weight_kernel, count),
        "weight_piece",
        [pl.BlockSpec(memory_space=pltpu.SMEM)]
        + in_vmem(2 + len(states))
        + [pl.BlockSpec(memory_space=pl.ANY)],
        [jax.ShapeDtypeStruct((NZ * unit, rows), bf16)],
        [pltpu.VMEM((rows, half), f32), pltpu.VMEM((half, rows), f32)],
    )(place, piece, squares, *states, after)[0]


def update_kernel(count, place_ref, own_ref, other_ref, squares_ref, *refs):
    states, outs, turned = refs[:3], refs[3:6], refs[6]
    y, c = place_ref[0], place_ref[1]
    half = turned.shape[0] // 2
    unit = half // NY
    for ref, core in ((own_ref, c), (other_ref, 1 - c)):
        for e in range(NY):
            at = pl.multiple_of(core * half + lax.rem(y + NY - e, NY) * unit, unit)
            turned[pl.ds(at, unit), :] = ref[e * unit : (e + 1) * unit, :].astype(f32)
    total = jnp.sum(squares_ref[:, :1])
    new = apply_update(turned[...].T, *[ref[...] for ref in states], total, count)
    for ref, value in zip(outs, new):
        ref[...] = value


def update(place, own, other, squares, states, count):
    rows, cols = states[0].shape
    return kernel_call(
        functools.partial(update_kernel, count),
        "update",
        [pl.BlockSpec(memory_space=pltpu.SMEM)] + in_vmem(3 + len(states)),
        [jax.ShapeDtypeStruct(states[0].shape, f32)] * 3,
        [pltpu.VMEM((cols, rows), f32)],
    )(place, own, other, squares, *states)


def add(*parts):
    total = parts[0].astype(f32)
    for part in parts[1:]:
        total = total + part.astype(f32)
    return total


def body(tokens, cotangent, master, first_moment, second_moment):
    y, c, x = lax.axis_index("y"), lax.axis_index("core"), lax.axis_index("x")
    place = jnp.stack([y, c, x]).astype(jnp.int32)
    states = (master, first_moment, second_moment)
    rows, cols = master.shape
    count = rows * NX * NZ * cols
    unit = cols // (NC * NY)

    own, other, held = partial_terms(place, cotangent, tokens)
    chip = {}
    for d in (2, 1, 3, 0):
        chip[d] = add(own[d], send(other[d], "core", 1)).astype(bf16)
    got = [routed(chip[d], d, True) for d in FAR_FIRST]
    line = add(chip[0], *got).astype(bf16)
    got = [routed(line[d * unit : (d + 1) * unit], d, False) for d in FAR_FIRST]
    plane = add(line[:unit], *got).astype(bf16)
    planes = lax.all_to_all(plane, "z", 1, 0, tiled=True)
    piece, squares = plane_sum(planes)
    grads = jnp.concatenate([piece] + [send(piece, "y", d) for d in (1, 2, 3)], 0)
    squares = lax.all_to_all(squares, NAMES, 0, 0, tiled=True)

    weight = weight_piece(place, piece, squares, states, grads, count)
    grads_other = send(grads, "core", 1)
    plane = lax.all_to_all(weight, "z", 0, 1, tiled=True)
    line = jnp.concatenate([plane] + [routed(plane, d, False) for d in (1, 2, 3)], 0)
    own = [line] + [routed(line, d, True) for d in (1, 2, 3)]
    other = [send(part, "core", 1) for part in own]

    master_new, first_new, second_new = update(place, grads, grads_other, squares, states, count)
    activations = forward(place, held, own, other)
    return (master_new, first_new, second_new, activations)


def solution(mesh):
    fine = Mesh(mesh.devices.reshape(NY, NC, NX, NZ), NAMES)
    by_token, by_row = P(NAMES, None), P(("x", "z"), None)
    return jax.shard_map(
        body,
        mesh=fine,
        in_specs=(by_token, by_token, by_row, by_row, by_row),
        out_specs=(by_row, by_row, by_row, by_token),
        check_vma=False,
    )
```

```python
import functools

import jax
import jax.numpy as jnp
from jax import lax
from jax.experimental import pallas as pl
from jax.experimental.pallas import tpu as pltpu
from jax.sharding import Mesh, PartitionSpec as P

STEP = 10

beta_first = 0.9
beta_second = 0.95
learn_rate = 0.02
decay_rate = 0.1
epsilon = 1e-08

NY, NC, NX, NZ = 4, 2, 4, 8
SIZE = {"y": NY, "core": NC, "x": NX, "z": NZ}
NAMES = ("y", "core", "x", "z")
f32 = jnp.float32
bf16 = jnp.bfloat16


def apply_update(grads, master, first, second, total, count):
    rms_value = jnp.sqrt(total / count)
    factor = 1.0 / jnp.maximum(rms_value, 1.0)
    clipped = grads * factor
    first_new = beta_first * first + (1.0 - beta_first) * clipped
    second_new = beta_second * second + (1.0 - beta_second) * clipped * clipped
    first_hat = first_new / (1.0 - beta_first**STEP)
    second_hat = second_new / (1.0 - beta_second**STEP)
    master_new = master - learn_rate * (
        first_hat / (jnp.sqrt(second_hat) + epsilon) + decay_rate * master
    )
    return (master_new, first_new, second_new)


def send(value, axis, step):
    n = SIZE[axis]
    return lax.ppermute(value, axis, [(i, (i + step) % n) for i in range(n)])


FAR_FIRST = (2, 1, 3)


def routed(value, step, first):
    pairs = []
    for y in range(NY):
        for c in range(NC):
            for x in range(NX):
                along_x = (c == 0) == first
                to_y, to_x = (y, (x + step) % NX) if along_x else ((y + step) % NY, x)
                pairs.append(((y * NC + c) * NX + x, (to_y * NC + c) * NX + to_x))
    return lax.ppermute(value, ("y", "core", "x"), pairs)


MIB = 2**20


def in_hbm(value):
    return pltpu.with_memory_space_constraint(value, pltpu.HBM)


def in_vmem(count):
    return [pl.BlockSpec(memory_space=pltpu.VMEM)] * count


def kernel_call(body, name, in_specs, out_shape, scratch=(), flops=0, moved=0, vmem=8 * MIB):
    return pl.pallas_call(
        body,
        in_specs=in_specs,
        out_specs=in_vmem(len(out_shape)),
        out_shape=out_shape,
        scratch_shapes=list(scratch),
        compiler_params=pltpu.CompilerParams(vmem_limit_bytes=vmem),
        cost_estimate=pl.CostEstimate(flops=flops, bytes_accessed=moved, transcendentals=0),
        name=name,
    )


def partial_kernel(place_ref, cot_ref, tokens_ref, *refs):
    own, other = refs[:NX], refs[NX : 2 * NX]
    held, cot, rows_t, rows, sems = refs[2 * NX :]
    y, c, x = place_ref[0], place_ref[1], place_ref[2]
    chunk = tokens_ref.shape[1] // NX
    half = rows.shape[0] // 2
    unit = half // NY
    cot_copy = pltpu.make_async_copy(cot_ref, cot, sems.at[NX])
    cot_copy.start()
    copies = []
    for d in range(NX):
        source = pl.multiple_of(lax.rem(x + d, NX) * chunk, chunk)
        copies.append(
            pltpu.make_async_copy(
                tokens_ref.at[:, pl.ds(source, chunk)],
                held.at[:, pl.ds(d * chunk, chunk)],
                sems.at[d],
            )
        )
        copies[-1].start()
    cot_copy.wait()
    rows_t[...] = cot[...].astype(f32).T.astype(bf16)
    for k, core in enumerate((c, 1 - c)):
        for e in range(NY):
            at = pl.multiple_of(core * half + lax.rem(y + e, NY) * unit, unit)
            rows[pl.ds(k * half + e * unit, unit), :] = rows_t[pl.ds(at, unit), :]

    for d in range(NX):
        copies[d].wait()

        def run(by_x, by_y):
            terms = jnp.dot(
                rows[...], held[:, d * chunk : (d + 1) * chunk], preferred_element_type=f32
            ).astype(bf16)
            mine, theirs = terms[:half], terms[half:]
            for_x, for_y = (mine, theirs) if by_x is own else (theirs, mine)
            by_x[d][...] = for_x
            for e in range(NY):
                by_y[e][d * unit : (d + 1) * unit, :] = for_y[e * unit : (e + 1) * unit]

        @pl.when(c == 0)
        def _():
            run(own, other)

        @pl.when(c == 1)
        def _():
            run(other, own)


def partial_terms(place, cotangent, tokens):
    count, width = tokens.shape
    cols = cotangent.shape[1]
    part = jax.ShapeDtypeStruct((cols // 2, width // NX), bf16)
    out = kernel_call(
        partial_kernel,
        "partial_terms",
        [
            pl.BlockSpec(memory_space=pltpu.SMEM),
            pl.BlockSpec(memory_space=pltpu.HBM),
            pl.BlockSpec(memory_space=pltpu.HBM),
        ],
        [part] * (2 * NX) + [pltpu.VMEM((count, width), bf16)],
        [
            pltpu.VMEM((count, cols), bf16),
            pltpu.VMEM((cols, count), bf16),
            pltpu.VMEM((cols, count), bf16),
            pltpu.SemaphoreType.DMA((NX + 1,)),
        ],
        2 * cols * count * width,
        2 * (count * width + cols * width + cols * count),
        16 * MIB,
    )(place, in_hbm(cotangent), in_hbm(tokens))
    return out[:NX], out[NX : 2 * NX], out[2 * NX]


def forward_kernel(place_ref, held, *refs):
    own, other = refs[:NX], refs[NX : 2 * NX]
    out_ref, weight, total = refs[2 * NX :]
    y, c = place_ref[0], place_ref[1]
    width = held.shape[1]
    chunk = width // NX
    half = weight.shape[1] // 2
    unit = half // NY

    def run(by_x, by_y):
        for d in range(NX):
            for e in range(NY):
                at = pl.multiple_of(lax.rem(y + NY - e, NY) * unit, unit)
                weight[d, pl.ds(at, unit), :] = by_x[d][e * unit : (e + 1) * unit, :]
                weight[d, pl.ds(half + at, unit), :] = by_y[e][d * unit : (d + 1) * unit, :]
            back = (NX - d) % NX
            terms = lax.dot_general(
                held[:, back * chunk : (back + 1) * chunk],
                weight[d],
                (((1,), (1,)), ((), ())),
                preferred_element_type=f32,
            )
            if d == 0:
                total[...] = terms
            else:
                total[...] += terms

    @pl.when(c == 0)
    def _():
        run(own, other)

    @pl.when(c == 1)
    def _():
        run(other, own)

    out_ref[...] = (total[...] * width ** (-0.5)).astype(bf16)


def forward(place, held, own, other):
    count, width = held.shape
    cols = 2 * own[0].shape[0]
    return kernel_call(
        forward_kernel,
        "forward",
        [pl.BlockSpec(memory_space=pltpu.SMEM)] + in_vmem(1 + 2 * NX),
        [jax.ShapeDtypeStruct((count, cols), bf16)],
        [pltpu.VMEM((NX, cols, width // NX), bf16), pltpu.VMEM((count, cols), f32)],
        2 * cols * count * width,
        2 * (count * width + cols * width + cols * count),
        16 * MIB,
    )(place, pltpu.with_memory_space_constraint(held, pltpu.VMEM), *own, *other)[0]


def plane_kernel(planes_ref, out_ref):
    unit = planes_ref.shape[0] // NZ
    total = planes_ref[:unit].astype(f32)
    for z in range(1, NZ):
        total += planes_ref[z * unit : (z + 1) * unit].astype(f32)
    piece = total.astype(bf16)
    for i in range(NC * NY):
        out_ref[i * unit : (i + 1) * unit, :] = piece


def plane_sum(planes):
    unit, rows = planes.shape[0] // NZ, planes.shape[1]
    shape = jax.ShapeDtypeStruct((NC * NY * unit, rows), bf16)
    return kernel_call(plane_kernel, "plane_sum", in_vmem(1), [shape])(planes)[0]


def square_kernel(grads_ref, squares_ref):
    grads = grads_ref[...].astype(f32)
    squares_ref[...] = jnp.broadcast_to(jnp.sum(grads * grads), squares_ref.shape)


def square_sum(grads):
    shape = jax.ShapeDtypeStruct((NX * NZ, 128), f32)
    return kernel_call(square_kernel, "square_sum", in_vmem(1), [shape])(grads)[0]


def weight_kernel(count, place_ref, grads_ref, squares_ref, *refs):
    states, (out_ref, turned) = refs[:3], refs[3:]
    y, c = place_ref[0], place_ref[1]
    half, rows = turned.shape
    unit = half // NY
    at = pl.multiple_of(c * half, half)
    lanes = pl.ds(at, half)
    total = jnp.sum(squares_ref[:, :1])
    grads = grads_ref[pl.ds(at, half), :].astype(f32).T
    new = apply_update(grads, *[state[:, lanes] for state in states], total, count)[0]
    turned[...] = new.T
    mine = turned[pl.ds(pl.multiple_of(y * unit, unit), unit), :].astype(bf16)
    for z in range(NZ):
        out_ref[z * unit : (z + 1) * unit, :] = mine


def weight_piece(place, grads, squares, states, count):
    rows, cols = states[0].shape
    return kernel_call(
        functools.partial(weight_kernel, count),
        "weight_piece",
        [pl.BlockSpec(memory_space=pltpu.SMEM)] + in_vmem(2 + len(states)),
        [jax.ShapeDtypeStruct((NZ * cols // (NC * NY), rows), bf16)],
        [pltpu.VMEM((cols // 2, rows), f32)],
    )(place, grads, squares, *states)[0]


def update_kernel(count, grads_ref, squares_ref, *refs):
    total = jnp.sum(squares_ref[:, :1])
    new = apply_update(grads_ref[...].astype(f32).T, *[ref[...] for ref in refs[:3]], total, count)
    for ref, value in zip(refs[3:], new):
        ref[...] = value


def update(grads, squares, states, count):
    return kernel_call(
        functools.partial(update_kernel, count),
        "update",
        in_vmem(2 + len(states)),
        [jax.ShapeDtypeStruct(states[0].shape, f32)] * 3,
    )(grads, squares, *states)


def add(*parts):
    total = parts[0].astype(f32)
    for part in parts[1:]:
        total = total + part.astype(f32)
    return total


def body(tokens, cotangent, master, first_moment, second_moment):
    y, c, x = lax.axis_index("y"), lax.axis_index("core"), lax.axis_index("x")
    place = jnp.stack([y, c, x]).astype(jnp.int32)
    states = (master, first_moment, second_moment)
    rows, cols = master.shape
    count = rows * NX * NZ * cols
    unit = cols // (NC * NY)

    own, other, held = partial_terms(place, cotangent, tokens)
    chip = {}
    for d in (2, 1, 3, 0):
        chip[d] = add(own[d], send(other[d], "core", 1)).astype(bf16)
    got = [routed(chip[d], d, True) for d in FAR_FIRST]
    line = add(chip[0], *got).astype(bf16)
    got = [routed(line[d * unit : (d + 1) * unit], d, False) for d in FAR_FIRST]
    plane = add(line[:unit], *got).astype(bf16)
    planes = lax.all_to_all(plane, "z", 1, 0, tiled=True)
    grads = lax.all_to_all(plane_sum(planes), ("core", "y"), 0, 0, tiled=True)
    squares = lax.all_to_all(square_sum(grads), ("x", "z"), 0, 0, tiled=True)

    weight = weight_piece(place, grads, squares, states, count)
    plane = lax.all_to_all(weight, "z", 0, 1, tiled=True)
    line = jnp.concatenate([plane] + [routed(plane, d, False) for d in (1, 2, 3)], 0)
    own = [line] + [routed(line, d, True) for d in (1, 2, 3)]
    other = [send(part, "core", 1) for part in own]

    master_new, first_new, second_new = update(grads, squares, states, count)
    activations = forward(place, held, own, other)
    return (master_new, first_new, second_new, activations)


def solution(mesh):
    fine = Mesh(mesh.devices.reshape(NY, NC, NX, NZ), NAMES)
    by_token, by_row = P(NAMES, None), P(("x", "z"), None)
    return jax.shard_map(
        body,
        mesh=fine,
        in_specs=(by_token, by_token, by_row, by_row, by_row),
        out_specs=(by_row, by_row, by_row, by_token),
        check_vma=False,
    )
```

```python
import functools

import jax
import jax.numpy as jnp
from jax import lax
from jax.experimental import pallas as pl
from jax.experimental.pallas import tpu as pltpu
from jax.sharding import Mesh, PartitionSpec as P

STEP = 10

beta_first = 0.9
beta_second = 0.95
learn_rate = 0.02
decay_rate = 0.1
epsilon = 1e-08

NY, NC, NX, NZ = 4, 2, 4, 8
SIZE = {"y": NY, "core": NC, "x": NX, "z": NZ}
NAMES = ("y", "core", "x", "z")
f32 = jnp.float32
bf16 = jnp.bfloat16


def apply_update(grads, master, first, second, total, count):
    rms_value = jnp.sqrt(total / count)
    factor = 1.0 / jnp.maximum(rms_value, 1.0)
    clipped = grads * factor
    first_new = beta_first * first + (1.0 - beta_first) * clipped
    second_new = beta_second * second + (1.0 - beta_second) * clipped * clipped
    first_hat = first_new / (1.0 - beta_first**STEP)
    second_hat = second_new / (1.0 - beta_second**STEP)
    master_new = master - learn_rate * (
        first_hat / (jnp.sqrt(second_hat) + epsilon) + decay_rate * master
    )
    return (master_new, first_new, second_new)


def send(value, axis, step):
    n = SIZE[axis]
    return lax.ppermute(value, axis, [(i, (i + step) % n) for i in range(n)])


FAR_FIRST = (2, 1, 3)


def routed(value, step, first):
    pairs = []
    for y in range(NY):
        for c in range(NC):
            for x in range(NX):
                along_x = (c == 0) == first
                to_y, to_x = (y, (x + step) % NX) if along_x else ((y + step) % NY, x)
                pairs.append(((y * NC + c) * NX + x, (to_y * NC + c) * NX + to_x))
    return lax.ppermute(value, ("y", "core", "x"), pairs)


MIB = 2**20
PARTS = 2


def in_hbm(value):
    return pltpu.with_memory_space_constraint(value, pltpu.HBM)


def in_vmem(count):
    return [pl.BlockSpec(memory_space=pltpu.VMEM)] * count


def kernel_call(body, name, in_specs, out_shape, scratch=(), flops=0, moved=0, vmem=8 * MIB):
    return pl.pallas_call(
        body,
        in_specs=in_specs,
        out_specs=in_vmem(len(out_shape)),
        out_shape=out_shape,
        scratch_shapes=list(scratch),
        compiler_params=pltpu.CompilerParams(vmem_limit_bytes=vmem),
        cost_estimate=pl.CostEstimate(flops=flops, bytes_accessed=moved, transcendentals=0),
        name=name,
    )


def partial_kernel(place_ref, cot_ref, tokens_ref, *refs):
    own, other = refs[:NX], refs[NX : 2 * NX]
    held, cot, rows_t, rows, sems = refs[2 * NX :]
    y, c, x = place_ref[0], place_ref[1], place_ref[2]
    chunk = tokens_ref.shape[1] // NX
    half = rows.shape[0] // 2
    unit = half // NY
    cot_copy = pltpu.make_async_copy(cot_ref, cot, sems.at[NX * PARTS])
    cot_copy.start()
    part = chunk // PARTS
    copies = []
    for d in range(NX):
        for h in range(PARTS):
            source = pl.multiple_of(lax.rem(x + d, NX) * chunk + h * part, part)
            copies.append(
                pltpu.make_async_copy(
                    tokens_ref.at[:, pl.ds(source, part)],
                    held.at[:, pl.ds(d * chunk + h * part, part)],
                    sems.at[d * PARTS + h],
                )
            )
            copies[-1].start()
    cot_copy.wait()
    rows_t[...] = cot[...].astype(f32).T.astype(bf16)
    for k, core in enumerate((c, 1 - c)):
        for e in range(NY):
            at = pl.multiple_of(core * half + lax.rem(y + e, NY) * unit, unit)
            rows[pl.ds(k * half + e * unit, unit), :] = rows_t[pl.ds(at, unit), :]

    for i in range(NX * PARTS):
        copies[i].wait()
        d, lanes = i // PARTS, slice(i % PARTS * part, (i % PARTS + 1) * part)

        def run(by_x, by_y):
            terms = jnp.dot(
                rows[...], held[:, i * part : (i + 1) * part], preferred_element_type=f32
            ).astype(bf16)
            mine, theirs = terms[:half], terms[half:]
            for_x, for_y = (mine, theirs) if by_x is own else (theirs, mine)
            by_x[d][:, lanes] = for_x
            for e in range(NY):
                by_y[e][d * unit : (d + 1) * unit, lanes] = for_y[e * unit : (e + 1) * unit]

        @pl.when(c == 0)
        def _():
            run(own, other)

        @pl.when(c == 1)
        def _():
            run(other, own)


def partial_terms(place, cotangent, tokens):
    count, width = tokens.shape
    cols = cotangent.shape[1]
    part = jax.ShapeDtypeStruct((cols // 2, width // NX), bf16)
    out = kernel_call(
        partial_kernel,
        "partial_terms",
        [
            pl.BlockSpec(memory_space=pltpu.SMEM),
            pl.BlockSpec(memory_space=pltpu.HBM),
            pl.BlockSpec(memory_space=pltpu.HBM),
        ],
        [part] * (2 * NX) + [pltpu.VMEM((count, width), bf16)],
        [
            pltpu.VMEM((count, cols), bf16),
            pltpu.VMEM((cols, count), bf16),
            pltpu.VMEM((cols, count), bf16),
            pltpu.SemaphoreType.DMA((NX * PARTS + 1,)),
        ],
        2 * cols * count * width,
        2 * (count * width + cols * width + cols * count),
        16 * MIB,
    )(place, in_hbm(cotangent), in_hbm(tokens))
    return out[:NX], out[NX : 2 * NX], out[2 * NX]


def forward_kernel(place_ref, held, *refs):
    own, other = refs[:NX], refs[NX : 2 * NX]
    out_ref, weight, total = refs[2 * NX :]
    y, c = place_ref[0], place_ref[1]
    width = held.shape[1]
    chunk = width // NX
    half = weight.shape[1] // 2
    unit = half // NY

    def run(by_x, by_y):
        for d in range(NX):
            for e in range(NY):
                at = pl.multiple_of(lax.rem(y + NY - e, NY) * unit, unit)
                weight[d, pl.ds(at, unit), :] = by_x[d][e * unit : (e + 1) * unit, :]
                weight[d, pl.ds(half + at, unit), :] = by_y[e][d * unit : (d + 1) * unit, :]
            back = (NX - d) % NX
            terms = lax.dot_general(
                held[:, back * chunk : (back + 1) * chunk],
                weight[d],
                (((1,), (1,)), ((), ())),
                preferred_element_type=f32,
            )
            if d == 0:
                total[...] = terms
            else:
                total[...] += terms

    @pl.when(c == 0)
    def _():
        run(own, other)

    @pl.when(c == 1)
    def _():
        run(other, own)

    out_ref[...] = (total[...] * width ** (-0.5)).astype(bf16)


def forward(place, held, own, other):
    count, width = held.shape
    cols = 2 * own[0].shape[0]
    return kernel_call(
        forward_kernel,
        "forward",
        [pl.BlockSpec(memory_space=pltpu.SMEM)] + in_vmem(1 + 2 * NX),
        [jax.ShapeDtypeStruct((count, cols), bf16)],
        [pltpu.VMEM((NX, cols, width // NX), bf16), pltpu.VMEM((count, cols), f32)],
        2 * cols * count * width,
        2 * (count * width + cols * width + cols * count),
        16 * MIB,
    )(place, pltpu.with_memory_space_constraint(held, pltpu.VMEM), *own, *other)[0]


def plane_kernel(planes_ref, out_ref):
    unit = planes_ref.shape[0] // NZ
    total = planes_ref[:unit].astype(f32)
    for z in range(1, NZ):
        total += planes_ref[z * unit : (z + 1) * unit].astype(f32)
    piece = total.astype(bf16)
    for i in range(NC * NY):
        out_ref[i * unit : (i + 1) * unit, :] = piece


def plane_sum(planes):
    unit, rows = planes.shape[0] // NZ, planes.shape[1]
    shape = jax.ShapeDtypeStruct((NC * NY * unit, rows), bf16)
    return kernel_call(plane_kernel, "plane_sum", in_vmem(1), [shape])(planes)[0]


def square_kernel(grads_ref, squares_ref):
    grads = grads_ref[...].astype(f32)
    squares_ref[...] = jnp.broadcast_to(jnp.sum(grads * grads), squares_ref.shape)


def square_sum(grads):
    shape = jax.ShapeDtypeStruct((NX * NZ, 128), f32)
    return kernel_call(square_kernel, "square_sum", in_vmem(1), [shape])(grads)[0]


def weight_kernel(count, place_ref, grads_ref, squares_ref, *refs):
    states, (out_ref, turned) = refs[:3], refs[3:]
    y, c = place_ref[0], place_ref[1]
    half, rows = turned.shape
    unit = half // NY
    at = pl.multiple_of(c * half, half)
    lanes = pl.ds(at, half)
    total = jnp.sum(squares_ref[:, :1])
    grads = grads_ref[pl.ds(at, half), :].astype(f32).T
    new = apply_update(grads, *[state[:, lanes] for state in states], total, count)[0]
    turned[...] = new.T
    mine = turned[pl.ds(pl.multiple_of(y * unit, unit), unit), :].astype(bf16)
    for z in range(NZ):
        out_ref[z * unit : (z + 1) * unit, :] = mine


def weight_piece(place, grads, squares, states, count):
    rows, cols = states[0].shape
    return kernel_call(
        functools.partial(weight_kernel, count),
        "weight_piece",
        [pl.BlockSpec(memory_space=pltpu.SMEM)] + in_vmem(2 + len(states)),
        [jax.ShapeDtypeStruct((NZ * cols // (NC * NY), rows), bf16)],
        [pltpu.VMEM((cols // 2, rows), f32)],
    )(place, grads, squares, *states)[0]


def update_kernel(count, grads_ref, squares_ref, *refs):
    total = jnp.sum(squares_ref[:, :1])
    new = apply_update(grads_ref[...].astype(f32).T, *[ref[...] for ref in refs[:3]], total, count)
    for ref, value in zip(refs[3:], new):
        ref[...] = value


def update(grads, squares, states, count):
    return kernel_call(
        functools.partial(update_kernel, count),
        "update",
        in_vmem(2 + len(states)),
        [jax.ShapeDtypeStruct(states[0].shape, f32)] * 3,
    )(grads, squares, *states)


def add(*parts):
    total = parts[0].astype(f32)
    for part in parts[1:]:
        total = total + part.astype(f32)
    return total


def body(tokens, cotangent, master, first_moment, second_moment):
    y, c, x = lax.axis_index("y"), lax.axis_index("core"), lax.axis_index("x")
    place = jnp.stack([y, c, x]).astype(jnp.int32)
    states = (master, first_moment, second_moment)
    rows, cols = master.shape
    count = rows * NX * NZ * cols
    unit = cols // (NC * NY)

    own, other, held = partial_terms(place, cotangent, tokens)
    chip = {}
    for d in (2, 1, 3, 0):
        chip[d] = add(own[d], send(other[d], "core", 1)).astype(bf16)
    got = [routed(chip[d], d, True) for d in FAR_FIRST]
    line = add(chip[0], *got).astype(bf16)
    got = [routed(line[d * unit : (d + 1) * unit], d, False) for d in FAR_FIRST]
    plane = add(line[:unit], *got).astype(bf16)
    planes = lax.all_to_all(plane, "z", 1, 0, tiled=True)
    grads = lax.all_to_all(plane_sum(planes), ("core", "y"), 0, 0, tiled=True)
    squares = lax.all_to_all(square_sum(grads), ("x", "z"), 0, 0, tiled=True)

    weight = weight_piece(place, grads, squares, states, count)
    plane = lax.all_to_all(weight, "z", 0, 1, tiled=True)
    line = jnp.concatenate([plane] + [routed(plane, d, False) for d in (1, 2, 3)], 0)
    own = [line] + [routed(line, d, True) for d in (1, 2, 3)]
    other = [send(part, "core", 1) for part in own]

    master_new, first_new, second_new = update(grads, squares, states, count)
    activations = forward(place, held, own, other)
    return (master_new, first_new, second_new, activations)


def solution(mesh):
    fine = Mesh(mesh.devices.reshape(NY, NC, NX, NZ), NAMES)
    by_token, by_row = P(NAMES, None), P(("x", "z"), None)
    return jax.shard_map(
        body,
        mesh=fine,
        in_specs=(by_token, by_token, by_row, by_row, by_row),
        out_specs=(by_row, by_row, by_row, by_token),
        check_vma=False,
    )
```

```python
import functools

import jax
import jax.numpy as jnp
from jax import lax
from jax.experimental import pallas as pl
from jax.experimental.pallas import tpu as pltpu
from jax.sharding import Mesh, PartitionSpec as P

STEP = 10

beta_first = 0.9
beta_second = 0.95
learn_rate = 0.02
decay_rate = 0.1
epsilon = 1e-08

NY, NC, NX, NZ = 4, 2, 4, 8
SIZE = {"y": NY, "core": NC, "x": NX, "z": NZ}
NAMES = ("y", "core", "x", "z")
f32 = jnp.float32
bf16 = jnp.bfloat16


def apply_update(grads, master, first, second, total, count):
    rms_value = jnp.sqrt(total / count)
    factor = 1.0 / jnp.maximum(rms_value, 1.0)
    clipped = grads * factor
    first_new = beta_first * first + (1.0 - beta_first) * clipped
    second_new = beta_second * second + (1.0 - beta_second) * clipped * clipped
    first_hat = first_new / (1.0 - beta_first**STEP)
    second_hat = second_new / (1.0 - beta_second**STEP)
    master_new = master - learn_rate * (
        first_hat / (jnp.sqrt(second_hat) + epsilon) + decay_rate * master
    )
    return (master_new, first_new, second_new)


def send(value, axis, step):
    n = SIZE[axis]
    return lax.ppermute(value, axis, [(i, (i + step) % n) for i in range(n)])


FAR_FIRST = (2, 1, 3)


def routed(value, step, first):
    pairs = []
    for y in range(NY):
        for c in range(NC):
            for x in range(NX):
                along_x = (c == 0) == first
                to_y, to_x = (y, (x + step) % NX) if along_x else ((y + step) % NY, x)
                pairs.append(((y * NC + c) * NX + x, (to_y * NC + c) * NX + to_x))
    return lax.ppermute(value, ("y", "core", "x"), pairs)


MIB = 2**20


def in_hbm(value):
    return pltpu.with_memory_space_constraint(value, pltpu.HBM)


def in_vmem(count):
    return [pl.BlockSpec(memory_space=pltpu.VMEM)] * count


def kernel_call(body, name, in_specs, out_shape, scratch=(), flops=0, moved=0, vmem=8 * MIB):
    return pl.pallas_call(
        body,
        in_specs=in_specs,
        out_specs=in_vmem(len(out_shape)),
        out_shape=out_shape,
        scratch_shapes=list(scratch),
        compiler_params=pltpu.CompilerParams(vmem_limit_bytes=vmem),
        cost_estimate=pl.CostEstimate(flops=flops, bytes_accessed=moved, transcendentals=0),
        name=name,
    )


def partial_kernel(place_ref, cot_ref, tokens_ref, *refs):
    own, other = refs[:NX], refs[NX : 2 * NX]
    held, cot, rows_t, rows, sems = refs[2 * NX :]
    y, c, x = place_ref[0], place_ref[1], place_ref[2]
    chunk = tokens_ref.shape[1] // NX
    half = rows.shape[0] // 2
    unit = half // NY
    cot_copy = pltpu.make_async_copy(cot_ref, cot, sems.at[NX])
    cot_copy.start()
    copies = []
    for d in range(NX):
        source = pl.multiple_of(lax.rem(x + d, NX) * chunk, chunk)
        copies.append(
            pltpu.make_async_copy(
                tokens_ref.at[:, pl.ds(source, chunk)],
                held.at[:, pl.ds(d * chunk, chunk)],
                sems.at[d],
            )
        )
        copies[-1].start()
    cot_copy.wait()
    rows_t[...] = cot[...].astype(f32).T.astype(bf16)
    for k, core in enumerate((c, 1 - c)):
        for e in range(NY):
            at = pl.multiple_of(core * half + lax.rem(y + e, NY) * unit, unit)
            rows[pl.ds(k * half + e * unit, unit), :] = rows_t[pl.ds(at, unit), :]

    for d in range(NX):
        copies[d].wait()

        def run(by_x, by_y):
            terms = jnp.dot(
                rows[...], held[:, d * chunk : (d + 1) * chunk], preferred_element_type=f32
            ).astype(bf16)
            mine, theirs = terms[:half], terms[half:]
            for_x, for_y = (mine, theirs) if by_x is own else (theirs, mine)
            by_x[d][...] = for_x
            for e in range(NY):
                by_y[e][d * unit : (d + 1) * unit, :] = for_y[e * unit : (e + 1) * unit]

        @pl.when(c == 0)
        def _():
            run(own, other)

        @pl.when(c == 1)
        def _():
            run(other, own)


def partial_terms(place, cotangent, tokens):
    count, width = tokens.shape
    cols = cotangent.shape[1]
    part = jax.ShapeDtypeStruct((cols // 2, width // NX), bf16)
    out = kernel_call(
        partial_kernel,
        "partial_terms",
        [
            pl.BlockSpec(memory_space=pltpu.SMEM),
            pl.BlockSpec(memory_space=pltpu.HBM),
            pl.BlockSpec(memory_space=pltpu.HBM),
        ],
        [part] * (2 * NX) + [pltpu.VMEM((count, width), bf16)],
        [
            pltpu.VMEM((count, cols), bf16),
            pltpu.VMEM((cols, count), bf16),
            pltpu.VMEM((cols, count), bf16),
            pltpu.SemaphoreType.DMA((NX + 1,)),
        ],
        2 * cols * count * width,
        2 * (count * width + cols * width + cols * count),
        16 * MIB,
    )(place, in_hbm(cotangent), in_hbm(tokens))
    return out[:NX], out[NX : 2 * NX], out[2 * NX]


def forward_kernel(place_ref, held, *refs):
    own, other = refs[:NX], refs[NX : 2 * NX]
    out_ref, weight, total = refs[2 * NX :]
    y, c = place_ref[0], place_ref[1]
    width = held.shape[1]
    chunk = width // NX
    half = weight.shape[1] // 2
    unit = half // NY

    def run(by_x, by_y):
        for d in range(NX):
            for e in range(NY):
                at = pl.multiple_of(lax.rem(y + NY - e, NY) * unit, unit)
                weight[d, pl.ds(at, unit), :] = by_x[d][e * unit : (e + 1) * unit, :]
                weight[d, pl.ds(half + at, unit), :] = by_y[e][d * unit : (d + 1) * unit, :]
            back = (NX - d) % NX
            terms = lax.dot_general(
                held[:, back * chunk : (back + 1) * chunk],
                weight[d],
                (((1,), (1,)), ((), ())),
                preferred_element_type=f32,
            )
            if d == 0:
                total[...] = terms
            else:
                total[...] += terms

    @pl.when(c == 0)
    def _():
        run(own, other)

    @pl.when(c == 1)
    def _():
        run(other, own)

    out_ref[...] = (total[...] * width ** (-0.5)).astype(bf16)


def forward(place, held, own, other):
    count, width = held.shape
    cols = 2 * own[0].shape[0]
    return kernel_call(
        forward_kernel,
        "forward",
        [pl.BlockSpec(memory_space=pltpu.SMEM)] + in_vmem(1 + 2 * NX),
        [jax.ShapeDtypeStruct((count, cols), bf16)],
        [pltpu.VMEM((NX, cols, width // NX), bf16), pltpu.VMEM((count, cols), f32)],
        2 * cols * count * width,
        2 * (count * width + cols * width + cols * count),
        16 * MIB,
    )(place, pltpu.with_memory_space_constraint(held, pltpu.VMEM), *own, *other)[0]


def plane_kernel(planes_ref, out_ref):
    unit = planes_ref.shape[0] // NZ
    total = planes_ref[:unit].astype(f32)
    for z in range(1, NZ):
        total += planes_ref[z * unit : (z + 1) * unit].astype(f32)
    piece = total.astype(bf16)
    for i in range(NC * NY):
        out_ref[i * unit : (i + 1) * unit, :] = piece


def plane_sum(planes):
    unit, rows = planes.shape[0] // NZ, planes.shape[1]
    shape = jax.ShapeDtypeStruct((NC * NY * unit, rows), bf16)
    return kernel_call(plane_kernel, "plane_sum", in_vmem(1), [shape])(planes)[0]


def square_kernel(grads_ref, squares_ref):
    grads = grads_ref[...].astype(f32)
    squares_ref[...] = jnp.broadcast_to(jnp.sum(grads * grads), squares_ref.shape)


def square_sum(grads):
    shape = jax.ShapeDtypeStruct((NX * NZ, 128), f32)
    return kernel_call(square_kernel, "square_sum", in_vmem(1), [shape])(grads)[0]


def weight_kernel(count, place_ref, grads_ref, squares_ref, *refs):
    states, (out_ref, turned) = refs[:3], refs[3:]
    y, c = place_ref[0], place_ref[1]
    half, rows = turned.shape
    unit = half // NY
    at = pl.multiple_of(c * half, half)
    lanes = pl.ds(at, half)
    total = jnp.sum(squares_ref[:, :1])
    grads = grads_ref[pl.ds(at, half), :].astype(f32).T
    new = apply_update(grads, *[state[:, lanes] for state in states], total, count)[0]
    turned[...] = new.T
    mine = turned[pl.ds(pl.multiple_of(y * unit, unit), unit), :].astype(bf16)
    for z in range(NZ):
        out_ref[z * unit : (z + 1) * unit, :] = mine


def weight_piece(place, grads, squares, states, count):
    rows, cols = states[0].shape
    return kernel_call(
        functools.partial(weight_kernel, count),
        "weight_piece",
        [pl.BlockSpec(memory_space=pltpu.SMEM)] + in_vmem(2 + len(states)),
        [jax.ShapeDtypeStruct((NZ * cols // (NC * NY), rows), bf16)],
        [pltpu.VMEM((cols // 2, rows), f32)],
    )(place, grads, squares, *states)[0]


def update_kernel(count, grads_ref, squares_ref, *refs):
    total = jnp.sum(squares_ref[:, :1])
    new = apply_update(grads_ref[...].astype(f32).T, *[ref[...] for ref in refs[:3]], total, count)
    for ref, value in zip(refs[3:], new):
        ref[...] = value


def update(grads, squares, states, count):
    return kernel_call(
        functools.partial(update_kernel, count),
        "update",
        in_vmem(2 + len(states)),
        [jax.ShapeDtypeStruct(states[0].shape, f32)] * 3,
    )(grads, squares, *states)


def add(*parts):
    total = parts[0].astype(f32)
    for part in parts[1:]:
        total = total + part.astype(f32)
    return total


def body(tokens, cotangent, master, first_moment, second_moment):
    y, c, x = lax.axis_index("y"), lax.axis_index("core"), lax.axis_index("x")
    place = jnp.stack([y, c, x]).astype(jnp.int32)
    states = (master, first_moment, second_moment)
    rows, cols = master.shape
    count = rows * NX * NZ * cols
    unit = cols // (NC * NY)

    own, other, held = partial_terms(place, cotangent, tokens)
    chip = {}
    for d in (2, 1, 3, 0):
        chip[d] = add(own[d], send(other[d], "core", 1)).astype(bf16)
    got = [routed(chip[d], d, True) for d in FAR_FIRST]
    line = add(chip[0], *got).astype(bf16)
    got = [routed(line[d * unit : (d + 1) * unit], d, False) for d in FAR_FIRST]
    plane = add(line[:unit], *got).astype(bf16)
    planes = lax.all_to_all(plane, "z", 1, 0, tiled=True)
    grads = lax.all_to_all(plane_sum(planes), ("core", "y"), 0, 0, tiled=True)
    squares = lax.all_to_all(square_sum(grads), ("x", "z"), 0, 0, tiled=True)

    weight = weight_piece(place, grads, squares, states, count)
    plane = lax.all_to_all(weight, "z", 0, 1, tiled=True)
    rest = jnp.concatenate([routed(plane, d, False) for d in (1, 2, 3)], 0)
    early = [plane] + [routed(plane, d, True) for d in (1, 2, 3)]
    late = [rest] + [routed(rest, d, True) for d in (1, 2, 3)]
    own = [jnp.concatenate(parts, 0) for parts in zip(early, late)]
    other = [send(part, "core", 1) for part in own]

    master_new, first_new, second_new = update(grads, squares, states, count)
    activations = forward(place, held, own, other)
    return (master_new, first_new, second_new, activations)


def solution(mesh):
    fine = Mesh(mesh.devices.reshape(NY, NC, NX, NZ), NAMES)
    by_token, by_row = P(NAMES, None), P(("x", "z"), None)
    return jax.shard_map(
        body,
        mesh=fine,
        in_specs=(by_token, by_token, by_row, by_row, by_row),
        out_specs=(by_row, by_row, by_row, by_token),
        check_vma=False,
    )
```
